256 devices in a mesh: flow: 32 (over z, x), lane: 8 (over y, core).
Axes of the slice: x: 4, y: 4, z: 8, core: 2. Of those that a mesh axis runs over, the one named last changes fastest.
Arguments:
- head_prev: float32 [16, 4, 64, 4096], P('lane', None, None, 'flow'), may hold values from -6 to 6
- storage: float32 [4, 64, 4096], P(None, None, 'flow'), may hold values from 6.1035157e-06 to 2.4414063e-05
- cond_flow: float32 [4, 64, 4096], P(None, None, 'flow'), may hold values from 0.5 to 2
- cond_cross: float32 [4, 64, 4096], P(None, None, 'flow'), may hold values from 6.1035157e-06 to 2.4414063e-05
- cond_vert: float32 [4, 64, 4096], P(None, None, 'flow'), may hold values from 6.1035157e-06 to 2.4414063e-05
- active: int32 [4, 64, 4096], P(None, None, 'flow'), may hold values from 0 to 1
- hru_cells: int32 [131072, 4], P('flow'), may hold values from 0 to 24575, as said below
- hru_area: float32 [131072, 4], P('flow'), may hold values from 0.1 to 1
- hru_land: int32 [131072], P('flow'), may hold values from 0 to 15
- hru_bmp: int32 [16, 131072], P('lane', 'flow'), may hold values from 0 to 7
- rain: float32 [131072], P('flow'), may hold values from 0.5 to 4
- perc_table: float32 [16, 8], replicated, may hold values from 6.1035157e-06 to 6.1035156e-05
- hru_live: int32 [32], P('flow'), may hold values from 1024 to 4096, as said below
Outputs:
- head: float32 [16, 4, 64, 4096], P('lane', None, None, 'flow')
- anomaly: float32 [16, 4, 64, 4096], P('lane', None, None, 'flow')
The draws below stay inside these ranges and needn't reach their ends.
Inputs may be any that keep to these rules, and one draw needn't show every extreme that they name: `hru_cells`: w // 8192 is 0 for the previous device along flow, 1 for the HRU's own device and 2 for the next; no target lies outside the grid. `hru_live`: slots of device k at positions 4096 * k + i with i at or above its count contribute nothing; some device is full.
All inputs are finite; a program needn't handle non-finite values.
Results may differ from the reference program's by a relative error of at most 0.00045.
Values sent between devices are 32-bit elements; how exact they have to be, the bound alone decides.
No kernel may reach another device: no remote copies, remote signals or barrier semaphores. Data moves between devices by JAX's collectives and lax.ppermute only.
A program may use at most 128 MiB of HBM per device.

```python
import math
import jax
import jax.numpy as jnp
from jax import lax

FLOW_DEV = 128
ACROSS = 64
LAYERS = 4
HRU_DEV = 4096
INTERSECTIONS = 4
LAND_USES = 16
PRACTICES = 8
SWEEPS = 2
NF = 4096
LANES = 16
HRUS = 131072
FLOW_DEVS = 32


def draw_active(key, part):
    key = jax.random.fold_in(key, 31)
    subkeys = jax.random.split(key, 6)
    left_base = jnp.maximum(jax.random.randint(subkeys[0], (1, ACROSS, 1), -FLOW_DEV, FLOW_DEV), 0)
    right_base = jnp.maximum(jax.random.randint(subkeys[1], (1, ACROSS, 1), -FLOW_DEV, FLOW_DEV), 0)
    deeper = FLOW_DEV // 4 + 1
    left_edge = left_base + jax.random.randint(subkeys[2], (LAYERS, ACROSS, 1), 0, deeper)
    right_edge = right_base + jax.random.randint(subkeys[3], (LAYERS, ACROSS, 1), 0, deeper)
    position = jnp.arange(NF, dtype=jnp.int32)[None, None, :]
    inside = (position >= left_edge) & (position < NF - right_edge)
    row_hit = jax.random.randint(subkeys[4], (LAYERS, ACROSS, 1), 0, 8) == 0
    spot = jax.random.randint(subkeys[5], (LAYERS, ACROSS, 1), 0, NF)
    inside = inside & jnp.logical_not(row_hit & (position == spot))
    flags = jnp.where(inside, 1, 0).astype(jnp.int32)
    flags = flags.at[0, 0, 0].set(0)
    flags = flags.at[LAYERS - 1, ACROSS - 1, NF // 2].set(1)
    return flags.astype(jnp.int32)


def draw_hru_cells(key, part):
    key = jax.random.fold_in(key, 11)
    subkeys = jax.random.split(key, 2)
    top_cells = ACROSS * FLOW_DEV
    chooser = jax.random.randint(subkeys[0], (HRUS, INTERSECTIONS), 0, 8)
    window_part = jnp.where(chooser == 0, 0, jnp.where(chooser == 7, 2, 1))
    owner_dev = (jnp.arange(HRUS, dtype=jnp.int32) // HRU_DEV)[:, None]
    window_part = jnp.where((owner_dev == 0) & (window_part == 0), 1, window_part)
    window_part = jnp.where((owner_dev == FLOW_DEVS - 1) & (window_part == 2), 1, window_part)
    target_cell = jax.random.randint(subkeys[1], (HRUS, INTERSECTIONS), 0, top_cells)
    result_cells = window_part * top_cells + target_cell
    result_cells = result_cells.at[0, 0].set(3 * top_cells - 1)
    result_cells = result_cells.at[HRU_DEV, 0].set(0)
    return result_cells.astype(jnp.int32)


def draw_hru_live(key, part):
    key = jax.random.fold_in(key, 23)
    subkeys = jax.random.split(key, 2)
    counts = jax.random.randint(subkeys[0], (FLOW_DEVS,), HRU_DEV // 4, HRU_DEV + 1)
    fuller = jax.random.randint(subkeys[1], (), 0, FLOW_DEVS)
    counts = jnp.where(jnp.arange(FLOW_DEVS, dtype=jnp.int32) == fuller, HRU_DEV, counts)
    return counts.astype(jnp.int32)


def touch_ends(array, rng, low, top_value):
    longest = array.shape.index(max(array.shape))
    spots = []
    for shift in (0, 1):
        where = [jax.random.randint(jax.random.fold_in(rng, axis), (), 0, length) for axis, length in enumerate(array.shape)]
        where[longest] = (where[longest] + shift) % array.shape[longest]
        spots.append(tuple(where))
    return array.at[spots[0]].set(low).at[spots[1]].set(top_value)


def level_of(key, dims, shards, least, high):
    level = 1.0
    for axis_at, shards_of in shards:
        draws = jax.random.uniform(jax.random.fold_in(jax.random.fold_in(key, 6), axis_at), (shards_of,), jnp.float32, least / len(shards), high / len(shards))
        level = level * jnp.repeat(jnp.exp(draws), dims[axis_at] // shards_of).reshape((-1,) + (1,) * (len(dims) - 1 - axis_at))
    return level


def bell_draw(stream_key, shape, deviation, limit, cuts=(), kind=jnp.bfloat16):
    level = level_of(stream_key, shape, cuts, -0.22, 0.18) if cuts else 1.0
    drawn = jax.random.normal(stream_key, shape, jnp.float32) * deviation * level
    return jnp.minimum(jnp.maximum(drawn, -limit), limit).astype(kind)


def setup_inputs(seed: int = 0) -> dict:
    arg_keys = jax.random.split(jax.random.key(seed), 14)
    return {
        "head_prev": bell_draw(arg_keys[0], (LANES, LAYERS, ACROSS, NF), 1.0, 6.0, ((0, 8), (3, 32)), jnp.float32),
        "storage": jnp.clip(jnp.exp(math.log(2.441406286379788e-05) - 1.3862944 * jax.random.uniform(arg_keys[1], (LAYERS, ACROSS, NF), jnp.float32) ** level_of(arg_keys[1], (LAYERS, ACROSS, NF), ((2, 32),), -0.2, 0.2)), 6.10351571594947e-06, 2.441406286379788e-05),
        "cond_flow": jnp.clip(jnp.exp(math.log(2.0) - 1.3862944 * jax.random.uniform(arg_keys[2], (LAYERS, ACROSS, NF), jnp.float32) ** level_of(arg_keys[2], (LAYERS, ACROSS, NF), ((2, 32),), -0.2, 0.2)), 0.5, 2.0),
        "cond_cross": jnp.clip(jnp.exp(math.log(2.441406286379788e-05) - 1.3862944 * jax.random.uniform(arg_keys[3], (LAYERS, ACROSS, NF), jnp.float32) ** level_of(arg_keys[3], (LAYERS, ACROSS, NF), ((2, 32),), -0.2, 0.2)), 6.10351571594947e-06, 2.441406286379788e-05),
        "cond_vert": jnp.clip(jnp.exp(math.log(2.441406286379788e-05) - 1.3862944 * jax.random.uniform(arg_keys[4], (LAYERS, ACROSS, NF), jnp.float32) ** level_of(arg_keys[4], (LAYERS, ACROSS, NF), ((2, 32),), -0.2, 0.2)), 6.10351571594947e-06, 2.441406286379788e-05),
        "active": draw_active(jax.random.fold_in(arg_keys[13], 71), 0),
        "hru_cells": draw_hru_cells(jax.random.fold_in(arg_keys[13], 71), 0),
        "hru_area": jnp.clip(0.1 + 0.9 * jax.random.uniform(arg_keys[7], (HRUS, INTERSECTIONS), jnp.float32) ** level_of(arg_keys[7], (HRUS, INTERSECTIONS), ((0, 32),), -0.2, 0.2), 0.1, 1.0),
        "hru_land": touch_ends(jax.random.randint(arg_keys[8], (HRUS,), 0, LAND_USES), jax.random.fold_in(arg_keys[8], 1), 0, LAND_USES - 1).astype(jnp.int32),
        "hru_bmp": touch_ends(jax.random.randint(arg_keys[9], (LANES, HRUS), 0, PRACTICES), jax.random.fold_in(arg_keys[9], 1), 0, PRACTICES - 1).astype(jnp.int32),
        "rain": jnp.clip(jnp.exp(math.log(4.0) - 2.0794415 * jax.random.uniform(arg_keys[10], (HRUS,), jnp.float32) ** level_of(arg_keys[10], (HRUS,), ((0, 32),), -0.2, 0.2)), 0.5, 4.0),
        "perc_table": jnp.clip(jnp.exp(jax.random.uniform(arg_keys[11], (LAND_USES, PRACTICES), jnp.float32, math.log(6.10351571594947e-06), math.log(6.103515625e-05))), 6.10351571594947e-06, 6.103515625e-05),
        "hru_live": draw_hru_live(jax.random.fold_in(arg_keys[13], 71), 0),
    }


def next_of(values, along):
    widths = [(0, 0)] * values.ndim
    widths[along] = (0, 1)
    return lax.slice_in_dim(jnp.pad(values, widths), 1, values.shape[along] + 1, axis=along)


def prev_of(values, along):
    widths = [(0, 0)] * values.ndim
    widths[along] = (1, 0)
    return lax.slice_in_dim(jnp.pad(values, widths), 0, values.shape[along], axis=along)


def line_solve(diagonal, face_lo, face_hi, rhs):
    shape = rhs.shape
    rows = tuple(jnp.moveaxis(jnp.broadcast_to(item, shape), -1, 0) for item in (diagonal, face_lo, face_hi, rhs))

    def forward(carry, row):
        ratio_prev, solved_prev = carry
        diag_row, lo_row, hi_row, rhs_row = row
        pivot = diag_row - lo_row * ratio_prev
        ratio = hi_row / pivot
        solved = (rhs_row + lo_row * solved_prev) / pivot
        return (ratio, solved), (ratio, solved)

    start = (jnp.zeros(shape[:-1], jnp.float32), jnp.zeros(shape[:-1], jnp.float32))
    _, (ratios, partial_rows) = lax.scan(forward, start, rows)

    def backward(after, row):
        ratio, solved = row
        result = solved + ratio * after
        return result, result

    _, results = lax.scan(backward, jnp.zeros(shape[:-1], jnp.float32), (ratios, partial_rows), reverse=True)
    return jnp.moveaxis(results, 0, -1)


def reference(head_prev, storage, cond_flow, cond_cross, cond_vert, active, hru_cells, hru_area, hru_land, hru_bmp, rain, perc_table, hru_live):
    cell_mask = active.astype(jnp.float32)
    flow_face = cond_flow * cell_mask * next_of(cell_mask, 2)
    cross_face = cond_cross * cell_mask * next_of(cell_mask, 1)
    vert_face = cond_vert * cell_mask * next_of(cell_mask, 0)
    flow_lo = prev_of(flow_face, 2)
    cross_lo = prev_of(cross_face, 1)
    vert_lo = prev_of(vert_face, 0)
    diagonal = storage + flow_lo + flow_face + cross_face + cross_lo + vert_face + vert_lo

    slot_index = jnp.arange(HRUS, dtype=jnp.int32)
    owner = slot_index // HRU_DEV
    live = ((slot_index % HRU_DEV) < hru_live[owner]).astype(jnp.float32)
    land_hot = (hru_land[:, None] == jnp.arange(LAND_USES, dtype=jnp.int32)[None]).astype(jnp.float32)
    rates = jnp.dot(land_hot, perc_table, precision=lax.Precision.HIGHEST)
    chosen = jnp.sum(jnp.where(hru_bmp[:, :, None] == jnp.arange(PRACTICES, dtype=jnp.int32)[None, None], rates[None], jnp.float32(0.0)), axis=2)
    perc = rain[None] * chosen * live[None]
    amounts = perc[:, :, None] * hru_area[None]
    top_cells = ACROSS * FLOW_DEV
    window_part = hru_cells // top_cells
    local_cell = hru_cells % top_cells
    cross_index = local_cell // FLOW_DEV
    flow_index = (owner[:, None] + window_part - 1) * FLOW_DEV + local_cell % FLOW_DEV
    recharge = jnp.zeros((LANES, ACROSS, NF), jnp.float32).at[:, cross_index, flow_index].add(amounts)
    recharge = recharge * cell_mask[0][None]

    head = head_prev
    for repeat in range(SWEEPS):
        rhs = storage[None] * head_prev
        rhs = rhs + cross_face[None] * next_of(head, 2) + cross_lo[None] * prev_of(head, 2)
        rhs = rhs + vert_face[None] * next_of(head, 1) + vert_lo[None] * prev_of(head, 1)
        rhs = rhs.at[:, 0].add(recharge)
        head = line_solve(diagonal, flow_lo, flow_face, rhs)
    anomaly = head - jnp.sum(head, axis=0, keepdims=True) / LANES
    return head, anomaly
```

```python
import functools

import jax
import jax.numpy as jnp
from jax import lax
from jax.experimental import pallas as pl
from jax.experimental.pallas import tpu as pltpu
from jax.sharding import PartitionSpec as P

STEPS = 16
SUBS = 8
ROWS = 24
F32 = jnp.float32


def halves(fn, a):
    return jnp.concatenate([fn(a[:, :128]), fn(a[:, 128:])], axis=1)


def cross_next(a):
    return halves(lambda h: pltpu.roll(h, 127, 1), a)


def cross_prev(a):
    return halves(lambda h: pltpu.roll(h, 1, 1), a)


def layer_rolls(a):
    lo = lax.broadcasted_iota(jnp.int32, (a.shape[0], 128), 1) < 64
    return lo, pltpu.roll(a[:, :128], 64, 1), pltpu.roll(a[:, 128:], 64, 1)


def layer_next(a):
    lo, r0, r1 = layer_rolls(a)
    return jnp.concatenate([jnp.where(lo, r0, r1), jnp.where(lo, r1, r0)], axis=1)


def layer_prev(a):
    lo, r0, r1 = layer_rolls(a)
    return jnp.concatenate([jnp.where(lo, r1, r0), jnp.where(lo, r0, r1)], axis=1)


def coupled(cross, vert, head):
    out = cross * cross_next(head) + cross_prev(cross * head)
    return out + vert * layer_next(head) + layer_prev(vert * head)


def reduce_chain(leak, face):
    n = len(leak)
    first, link, shunt = leak[0], face[0], leak[1]
    inv, ratio, share = [None] * n, [None] * n, [None] * n
    for i in range(1, n - 1):
        inv[i] = 1.0 / (face[i] + (shunt + link))
        ratio[i] = face[i] * inv[i]
        share[i] = link * inv[i]
        first = first + shunt * share[i]
        shunt = leak[i + 1] + shunt * ratio[i]
        link = link * ratio[i]
    return (inv, ratio, share), first, shunt, link


def reduce_source(ratio, share, rhs):
    n = len(rhs)
    first = rhs[0]
    part = [None] * n
    part[1] = rhs[1]
    for i in range(1, n - 1):
        first = first + share[i] * part[i]
        part[i + 1] = rhs[i + 1] + ratio[i] * part[i]
    return part, first, part[n - 1]


def fill_chain(coef, part, first, last):
    inv, ratio, share = coef
    n = len(ratio)
    out = [None] * n
    out[0], out[n - 1] = first, last
    for i in range(n - 2, 0, -1):
        value = share[i] * first + ratio[i] * out[i + 1]
        out[i] = value if part is None else value + inv[i] * part[i]
    return out


def full_factor(leak, face):
    n = len(leak)
    shunt = leak[0]
    inv, ratio = [None] * n, [None] * n
    for i in range(n - 1):
        inv[i] = 1.0 / (face[i] + shunt)
        ratio[i] = face[i] * inv[i]
        shunt = leak[i + 1] + shunt * ratio[i]
    inv[n - 1] = 1.0 / shunt
    return inv, ratio


def full_solve(inv, ratio, rhs):
    n = len(rhs)
    part = [rhs[0]]
    for i in range(n - 1):
        part.append(rhs[i + 1] + ratio[i] * part[i])
    out = [None] * n
    out[n - 1] = inv[n - 1] * part[n - 1]
    for i in range(n - 2, -1, -1):
        out[i] = inv[i] * part[i] + ratio[i] * out[i + 1]
    return out


def to_rows(a):
    return [a[k : k + 1] for k in range(SUBS)]


def interleave(a, b):
    return [x for pair in zip(to_rows(a), to_rows(b)) for x in pair]


def stack_ends(nodes):
    return jnp.concatenate(nodes[0::2], axis=0), jnp.concatenate(nodes[1::2], axis=0)


def column_sum(a):
    return jnp.sum(a, axis=0, keepdims=True)


def both(fn):
    return jnp.concatenate([fn(0), fn(1)], axis=1)


def step_rows(i):
    return pl.ds(i, SUBS, stride=STEPS)


def scatter_kernel(cells_ref, area_ref, land_ref, bmp_ref, rain_ref, table_ref, live_ref,
                   before_ref, own_ref, after_ref, amount_ref, acc_ref):
    slots = land_ref.shape[1]
    land = land_ref[...]
    rates = jnp.zeros((8, slots), F32)
    for use in range(table_ref.shape[1]):
        rates = jnp.where(land == use, table_ref[:, use : use + 1], rates)
    bmp = bmp_ref[...]
    chosen = jnp.zeros(bmp.shape, F32)
    for code in range(table_ref.shape[0]):
        chosen = jnp.where(bmp == code, rates[code : code + 1], chosen)
    alive = lax.broadcasted_iota(jnp.int32, (1, slots), 1) < live_ref[0]
    perc = jnp.where(alive, rain_ref[...] * chosen, 0.0)
    for q in range(4):
        amount = perc * area_ref[q : q + 1, :]
        high = amount.astype(jnp.bfloat16).astype(F32)
        amount_ref[q, 0:2, :] = high
        amount_ref[q, 2:4, :] = amount - high
    acc_ref[...] = jnp.zeros_like(acc_ref)
    width = 1024
    column = lax.broadcasted_iota(jnp.int32, (128, width), 0)
    line = lax.broadcasted_iota(jnp.int32, (192, width), 0)
    for q in range(4):

        @pl.loop(0, slots // width)
        def _(c):
            at = pl.ds(pl.multiple_of(c * width, width), width)
            cell = cells_ref[q : q + 1, at]
            hit = column == (cell & 127)
            put = [jnp.where(hit, amount_ref[q, k : k + 1, at], 0.0).astype(jnp.bfloat16) for k in (0, 2, 1, 3)]
            rows = jnp.where(line == (cell >> 7), 1.0, 0.0).astype(jnp.bfloat16)
            acc_ref[...] += lax.dot_general(
                jnp.concatenate(put, axis=0), rows, (((1,), (1,)), ((), ())), preferred_element_type=F32
            )

    lane0 = acc_ref[0:128, :] + acc_ref[128:256, :]
    lane1 = acc_ref[256:384, :] + acc_ref[384:512, :]
    for k, ref in enumerate((before_ref, own_ref, after_ref)):
        ref[...] = jnp.concatenate([lane0[:, 64 * k : 64 * k + 64], lane1[:, 64 * k : 64 * k + 64]], axis=1)


def coefficient_kernel(head_ref, storage_ref, flow_ref, cross_ref, vert_ref, active_ref,
                       fields_ref, small_ref, base_ref, gather_ref, turned):
    def turn(slot, part):
        for h in range(2):
            turned[slot, h] = part(h).T

    for slot, ref in enumerate((storage_ref, flow_ref, cross_ref, vert_ref)):
        turn(slot, lambda h: ref[2 * h : 2 * h + 2].reshape(128, 128))
    turn(4, lambda h: active_ref[2 * h : 2 * h + 2].reshape(128, 128).astype(F32))
    for s in range(2):
        turn(5 + s, lambda h: head_ref[s, 2 * h : 2 * h + 2].reshape(128, 128))

    def step(slot, i):
        return both(lambda h: turned[slot, h, step_rows(i), :])

    lane = lax.broadcasted_iota(jnp.int32, (SUBS, 256), 1)
    inner_cross = lane % 64 != 63
    inner_vert = lane < 192
    mask = [step(4, i) for i in range(STEPS)]
    leak, face, crosses, verts = [], [], [], []
    for i in range(STEPS):
        m = mask[i]
        cross = jnp.where(inner_cross, step(2, i) * m * cross_next(m), 0.0)
        vert = jnp.where(inner_vert, step(3, i) * m * layer_next(m), 0.0)
        store = step(0, i)
        leak.append(store + cross + cross_prev(cross) + vert + layer_prev(vert))
        after = mask[i + 1] if i + 1 < STEPS else pltpu.roll(mask[0], SUBS - 1, 0)
        face.append(step(1, i) * m * after)
        crosses.append(cross)
        verts.append(vert)
        fields_ref[0, i] = cross
        fields_ref[1, i] = vert
        fields_ref[2, i] = m
        for s in range(2):
            head = step(5 + s, i)
            base = store * head
            base_ref[s, i] = base
            base_ref[2 + s, i] = base + coupled(cross, vert, head)
    coef, first, last, link = reduce_chain(leak, face[: STEPS - 1])
    leak1 = interleave(first, last)
    face1 = interleave(link, face[STEPS - 1])[: 2 * SUBS - 1]
    coef1, first1, last1, link1 = reduce_chain(leak1, face1)
    for k in range(3):
        for i in range(1, STEPS - 1):
            fields_ref[3 + k, i] = coef[k][i]
        for i in range(1, 2 * SUBS - 1):
            small_ref[k, i : i + 1] = coef1[k][i]
    one, zero = jnp.ones((1, 256), F32), jnp.zeros((1, 256), F32)
    basis = []
    for ends in ((one, zero), (zero, one)):
        basis.append(fill_chain(coef, None, *stack_ends(fill_chain(coef1, None, *ends))))
    for k in range(2):
        for i in range(STEPS):
            fields_ref[6 + k, i] = basis[k][i]
    gather_ref[0:1] = first1
    gather_ref[1:2] = last1
    gather_ref[2:3] = link1
    gather_ref[3:4] = both(lambda h: turned[1, h, 127:128, :] * turned[4, h, 127:128, :])
    gather_ref[4:5] = both(lambda h: turned[4, h, 0:1, :])
    for row, weight, move in ((5, crosses, cross_next), (9, verts, layer_next)):
        sums = [jnp.zeros((SUBS, 256), F32)] * 4
        for i in range(STEPS):
            moved = [move(basis[k][i]) for k in range(2)]
            for a in range(2):
                weighted = weight[i] * basis[a][i]
                for b in range(2):
                    sums[2 * a + b] = sums[2 * a + b] + weighted * moved[b]
        for k in range(4):
            gather_ref[row + k : row + k + 1] = column_sum(sums[k])


def load_coef(fields_ref, small_ref):
    coef = tuple([None] + [fields_ref[3 + k, i] for i in range(1, STEPS - 1)] + [None] for k in range(3))
    coef1 = tuple([None] + [small_ref[k, i : i + 1] for i in range(1, 2 * SUBS - 1)] + [None] for k in range(3))
    return coef, coef1


def local_solve(coef, coef1, rhs, first, last):
    part, ends_first, ends_last = reduce_source(coef[1], coef[2], rhs)
    part1, source_first, source_last = reduce_source(coef1[1], coef1[2], interleave(ends_first, ends_last))
    ends = stack_ends(fill_chain(coef1, part1, first, last))
    return fill_chain(coef, part, *ends), source_first, source_last


def source_kernel(fields_ref, small_ref, base_ref, own_ref, low_ref, high_ref, coefs_ref,
                  source_ref, inner_ref, out_ref, rain_scratch):
    rain_scratch[...] = own_ref[...] + low_ref[...] + high_ref[...]
    coef, coef1 = load_coef(fields_ref, small_ref)
    top = lax.broadcasted_iota(jnp.int32, (SUBS, 128), 1) < 64
    zero = jnp.zeros((1, 256), F32)
    none = jnp.zeros((SUBS, 128), F32)
    rows = []
    for s in range(2):
        rhs = []
        for i in range(STEPS):
            water = rain_scratch[step_rows(i), :]
            if s:
                water = pltpu.roll(water, 64, 1)
            water = jnp.concatenate([jnp.where(top, water, 0.0), none], axis=1) * fields_ref[2, i]
            source_ref[s, i] = base_ref[s, i] + water
            rhs.append(base_ref[2 + s, i] + water)
        inner, first, last = local_solve(coef, coef1, rhs, zero, zero)
        sums = [jnp.zeros((SUBS, 256), F32)] * 2
        for i in range(STEPS):
            inner_ref[s, i] = inner[i]
            later = source_ref[s, i] + coupled(fields_ref[0, i], fields_ref[1, i], inner[i])
            for k in range(2):
                sums[k] = sums[k] + fields_ref[6 + k, i] * later
        rows += [first, last, column_sum(sums[0]), column_sum(sums[1])]
    head = coefs_ref[0:13]
    block = jnp.concatenate([head] + rows + [jnp.zeros((3, 256), F32)], axis=0)
    for k in range(out_ref.shape[0]):
        for h in range(2):
            out_ref[k, ROWS * h : ROWS * h + ROWS] = block[:, 128 * h : 128 * h + 128]


def sweep_kernel(place_ref, gathered_ref, fields_ref, small_ref, source_ref, inner_ref,
                 head_ref, total_ref, ends_scratch, turned):
    devices = gathered_ref.shape[0] // (2 * ROWS)
    per = devices // SUBS

    def got(row, i):
        return both(lambda h: gathered_ref[pl.ds((2 * i + h) * ROWS + row, SUBS, stride=2 * per * ROWS), :])

    leak, face = [], []
    for i in range(per):
        leak += [got(0, i), got(1, i)]
        after = got(4, i + 1) if i + 1 < per else pltpu.roll(got(4, 0), SUBS - 1, 0)
        face += [got(2, i), got(3, i) * after]
    coef, first, last, link = reduce_chain(leak, face[: 2 * per - 1])
    leak1 = interleave(first, last)
    face1 = interleave(link, face[2 * per - 1])[: 2 * SUBS - 1]
    inv1, ratio1 = full_factor(leak1, face1)

    def across_devices(rhs):
        part, ends_first, ends_last = reduce_source(coef[1], coef[2], rhs)
        ends = full_solve(inv1, ratio1, interleave(ends_first, ends_last))
        return fill_chain(coef, part, *stack_ends(ends))

    cross_k = [[got(5 + k, i) for k in range(4)] for i in range(per)]
    vert_k = [[got(9 + k, i) for k in range(4)] for i in range(per)]
    for s in range(2):
        row = 13 + 4 * s
        ends = across_devices([got(row + a, i) for i in range(per) for a in range(2)])
        rhs = []
        for i in range(per):
            low, high = ends[2 * i], ends[2 * i + 1]
            later = [got(row + 2 + a, i) for a in range(2)]
            for k, ahead, back in ((cross_k[i], cross_next, cross_prev), (vert_k[i], layer_next, layer_prev)):
                low_ahead, high_ahead = ahead(low), ahead(high)
                later[0] = later[0] + k[0] * low_ahead + k[1] * high_ahead + back(k[0] * low + k[2] * high)
                later[1] = later[1] + k[2] * low_ahead + k[3] * high_ahead + back(k[1] * low + k[3] * high)
            rhs += later
        ends2 = across_devices(rhs)
        for i in range(per):
            for k, value in enumerate((ends[2 * i], ends[2 * i + 1], ends2[2 * i], ends2[2 * i + 1])):
                ends_scratch[4 * s + k, SUBS * i : SUBS * i + SUBS] = value
    coef, coef1 = load_coef(fields_ref, small_ref)
    place = place_ref[0]
    at = pl.ds((place % per) * SUBS + place // per, 1)
    for s in range(2):
        low1, high1, low2, high2 = [ends_scratch[4 * s + k, at, :] for k in range(4)]
        rhs = []
        for i in range(STEPS):
            head = inner_ref[s, i] + fields_ref[6, i] * low1 + fields_ref[7, i] * high1
            rhs.append(source_ref[s, i] + coupled(fields_ref[0, i], fields_ref[1, i], head))
        solved, _, _ = local_solve(coef, coef1, rhs, low2, high2)
        for i in range(STEPS):
            for h in range(2):
                turned[s, h, step_rows(i), :] = solved[i][:, 128 * h : 128 * h + 128]
    for h in range(2):
        lanes = [turned[s, h].T for s in range(2)]
        for s in range(2):
            head_ref[s, 2 * h : 2 * h + 2] = lanes[s].reshape(2, 64, 128)
        total_ref[2 * h : 2 * h + 2] = (lanes[0] + lanes[1]).reshape(2, 64, 128)


VMEM = pl.BlockSpec(memory_space=pltpu.VMEM)
SMEM = pl.BlockSpec(memory_space=pltpu.SMEM)


def kernel_call(body, name, specs, outs, scratch, flops):
    return pl.pallas_call(
        body,
        name=name,
        in_specs=specs,
        out_specs=[VMEM] * len(outs),
        out_shape=[jax.ShapeDtypeStruct(shape, F32) for shape in outs],
        scratch_shapes=[pltpu.VMEM(shape, F32) for shape in scratch],
        compiler_params=pltpu.CompilerParams(vmem_limit_bytes=48 * 2**20),
        cost_estimate=pl.CostEstimate(flops=flops, bytes_accessed=2 * 2**20, transcendentals=0),
    )


def on_device(
    head_prev,
    storage,
    cond_flow,
    cond_cross,
    cond_vert,
    active,
    hru_cells,
    hru_area,
    hru_land,
    hru_bmp,
    rain,
    perc_table,
    hru_live,
):
    slots = hru_land.shape[0]
    devices = lax.axis_size("flow")
    tile = (128, 128)
    before, own, after = kernel_call(
        scatter_kernel, "scatter", [VMEM] * 6 + [SMEM], [tile] * 3, [(4, 4, slots), (512, 192)], 4 * 10**9
    )(
        hru_cells.T, hru_area.T, hru_land.reshape(1, slots), hru_bmp, rain.reshape(1, slots), perc_table.T, hru_live
    )
    high = lax.ppermute(before, "flow", [(i + 1, i) for i in range(devices - 1)])
    low = lax.ppermute(after, "flow", [(i, i + 1) for i in range(devices - 1)])
    fields, small, base, coefs = kernel_call(
        coefficient_kernel,
        "coefficients",
        [VMEM] * 6,
        [(8, STEPS, SUBS, 256), (3, 2 * SUBS, 256), (4, STEPS, SUBS, 256), (16, 256)],
        [(7, 2, 128, 128)],
        4 * 10**9,
    )(head_prev, storage, cond_flow, cond_cross, cond_vert, active)
    source, inner, block = kernel_call(
        source_kernel,
        "sources",
        [VMEM] * 7,
        [(2, STEPS, SUBS, 256), (2, STEPS, SUBS, 256), (devices, 2 * ROWS, 128)],
        [tile],
        10**9,
    )(fields, small, base, own, low, high, coefs)
    gathered = lax.all_to_all(block, "flow", split_axis=0, concat_axis=0, tiled=True)
    place = lax.axis_index("flow").astype(jnp.int32).reshape(1)
    head, total = kernel_call(
        sweep_kernel,
        "sweeps",
        [SMEM] + [VMEM] * 5,
        [head_prev.shape, storage.shape],
        [(8, devices, 256), (2, 2, 128, 128)],
        10**9,
    )(place, gathered.reshape(devices * 2 * ROWS, 128), fields, small, source, inner)
    lanes = lax.axis_size("lane")
    total = total + lax.ppermute(total, "lane", [(i, i ^ 1) for i in range(lanes)])
    whole = total
    for k in range(2, lanes, 2):
        whole = whole + lax.ppermute(total, "lane", [(i, (i + k) % lanes) for i in range(lanes)])
    anomaly = head - whole[None] / (2 * lanes)
    return head, anomaly


def solution(mesh):
    return jax.shard_map(
        on_device,
        mesh=mesh,
        in_specs=(
            P("lane", None, None, "flow"),
            P(None, None, "flow"),
            P(None, None, "flow"),
            P(None, None, "flow"),
            P(None, None, "flow"),
            P(None, None, "flow"),
            P("flow", None),
            P("flow", None),
            P("flow"),
            P("lane", "flow"),
            P("flow"),
            P(),
            P("flow"),
        ),
        out_specs=(P("lane", None, None, "flow"), P("lane", None, None, "flow")),
        check_vma=False,
    )
```

```python
import functools

import jax
import jax.numpy as jnp
from jax import lax
from jax.experimental import pallas as pl
from jax.experimental.pallas import tpu as pltpu
from jax.sharding import PartitionSpec as P

STEPS = 16
SUBS = 8
ROWS = 24
F32 = jnp.float32
BF16 = jnp.bfloat16


def halves(fn, a):
    return jnp.concatenate([fn(a[:, :128]), fn(a[:, 128:])], axis=1)


def cross_next(a):
    return halves(lambda h: pltpu.roll(h, 127, 1), a)


def cross_prev(a):
    return halves(lambda h: pltpu.roll(h, 1, 1), a)


def layer_rolls(a):
    lo = lax.broadcasted_iota(jnp.int32, (a.shape[0], 128), 1) < 64
    return lo, pltpu.roll(a[:, :128], 64, 1), pltpu.roll(a[:, 128:], 64, 1)


def layer_next(a):
    lo, r0, r1 = layer_rolls(a)
    return jnp.concatenate([jnp.where(lo, r0, r1), jnp.where(lo, r1, r0)], axis=1)


def layer_prev(a):
    lo, r0, r1 = layer_rolls(a)
    return jnp.concatenate([jnp.where(lo, r1, r0), jnp.where(lo, r0, r1)], axis=1)


def coupled(cross, vert, head):
    out = cross * cross_next(head) + cross_prev(cross * head)
    return out + vert * layer_next(head) + layer_prev(vert * head)


def reduce_chain(leak, face):
    n = len(leak)
    first, link, shunt = leak[0], face[0], leak[1]
    inv, ratio, share = [None] * n, [None] * n, [None] * n
    for i in range(1, n - 1):
        inv[i] = 1.0 / (face[i] + (shunt + link))
        ratio[i] = face[i] * inv[i]
        share[i] = link * inv[i]
        first = first + shunt * share[i]
        shunt = leak[i + 1] + shunt * ratio[i]
        link = link * ratio[i]
    return (inv, ratio, share), first, shunt, link


def reduce_source(ratio, share, rhs):
    n = len(rhs)
    first = rhs[0]
    part = [None] * n
    part[1] = rhs[1]
    for i in range(1, n - 1):
        first = first + share[i] * part[i]
        part[i + 1] = rhs[i + 1] + ratio[i] * part[i]
    return part, first, part[n - 1]


def fill_chain(coef, part, first, last):
    inv, ratio, share = coef
    n = len(ratio)
    out = [None] * n
    out[0], out[n - 1] = first, last
    for i in range(n - 2, 0, -1):
        value = share[i] * first + ratio[i] * out[i + 1]
        out[i] = value if part is None else value + inv[i] * part[i]
    return out


def full_factor(leak, face):
    n = len(leak)
    shunt = leak[0]
    inv, ratio = [None] * n, [None] * n
    for i in range(n - 1):
        inv[i] = 1.0 / (face[i] + shunt)
        ratio[i] = face[i] * inv[i]
        shunt = leak[i + 1] + shunt * ratio[i]
    inv[n - 1] = 1.0 / shunt
    return inv, ratio


def full_solve(inv, ratio, rhs):
    n = len(rhs)
    part = [rhs[0]]
    for i in range(n - 1):
        part.append(rhs[i + 1] + ratio[i] * part[i])
    out = [None] * n
    out[n - 1] = inv[n - 1] * part[n - 1]
    for i in range(n - 2, -1, -1):
        out[i] = inv[i] * part[i] + ratio[i] * out[i + 1]
    return out


def to_rows(a):
    return [a[k : k + 1] for k in range(SUBS)]


def interleave(a, b):
    return [x for pair in zip(to_rows(a), to_rows(b)) for x in pair]


def stack_ends(nodes):
    return jnp.concatenate(nodes[0::2], axis=0), jnp.concatenate(nodes[1::2], axis=0)


def column_sum(a):
    return jnp.sum(a, axis=0, keepdims=True)


def both(fn):
    return jnp.concatenate([fn(0), fn(1)], axis=1)


def step_rows(i):
    return pl.ds(i, SUBS, stride=STEPS)


def scatter_kernel(cells_ref, area_ref, land_ref, bmp_ref, rain_ref, table_ref, live_ref,
                   before_ref, own_ref, after_ref, amount_ref, window_ref):
    slots = land_ref.shape[1]
    land = land_ref[...]
    rates = jnp.zeros((8, slots), F32)
    for use in range(table_ref.shape[1]):
        rates = jnp.where(land == use, table_ref[:, use : use + 1], rates)
    bmp = bmp_ref[...]
    chosen = jnp.zeros(bmp.shape, F32)
    for code in range(table_ref.shape[0]):
        chosen = jnp.where(bmp == code, rates[code : code + 1], chosen)
    alive = lax.broadcasted_iota(jnp.int32, (1, slots), 1) < live_ref[0]
    perc = jnp.where(alive, rain_ref[...] * chosen, 0.0)
    for q in range(4):
        amount = perc * area_ref[q : q + 1, :]
        high = amount.astype(BF16).astype(F32)
        amount_ref[q, 0:2, :] = high
        amount_ref[q, 2:4, :] = amount - high
    column = lax.broadcasted_iota(jnp.int32, (256, slots), 0).astype(F32).astype(BF16)
    line = lax.broadcasted_iota(jnp.int32, (96, slots), 0).astype(F32).astype(BF16)
    one, zero = jnp.ones((), BF16), jnp.zeros((), BF16)
    total = None
    for q in range(4):
        cell = cells_ref[q : q + 1, :]
        columns = jnp.where(column == (cell & 255).astype(F32).astype(BF16), one, zero)
        hit = line == (cell >> 8).astype(F32).astype(BF16)
        put = [jnp.where(hit, amount_ref[q, k : k + 1, :].astype(BF16), zero) for k in (0, 2, 1, 3)]
        product = lax.dot_general(
            jnp.concatenate(put, axis=0), columns, (((1,), (1,)), ((), ())), preferred_element_type=F32
        )
        total = product if total is None else total + product
    for s in range(2):
        summed = total[192 * s : 192 * s + 96] + total[192 * s + 96 : 192 * s + 192]
        for k in range(3):
            for odd in range(2):
                window_ref[k, pl.ds(64 * s + odd, 32, stride=2), :] = summed[
                    32 * k : 32 * k + 32, 128 * odd : 128 * odd + 128
                ]
    for k, ref in enumerate((before_ref, own_ref, after_ref)):
        ref[...] = window_ref[k].T


def coefficient_kernel(head_ref, storage_ref, flow_ref, cross_ref, vert_ref, active_ref,
                       fields_ref, small_ref, base_ref, gather_ref, turned):
    def turn(slot, part):
        for h in range(2):
            turned[slot, h] = part(h).T

    for slot, ref in enumerate((storage_ref, flow_ref, cross_ref, vert_ref)):
        turn(slot, lambda h: ref[2 * h : 2 * h + 2].reshape(128, 128))
    turn(4, lambda h: active_ref[2 * h : 2 * h + 2].reshape(128, 128).astype(F32))
    for s in range(2):
        turn(5 + s, lambda h: head_ref[s, 2 * h : 2 * h + 2].reshape(128, 128))

    def step(slot, i):
        return both(lambda h: turned[slot, h, step_rows(i), :])

    lane = lax.broadcasted_iota(jnp.int32, (SUBS, 256), 1)
    inner_cross = lane % 64 != 63
    inner_vert = lane < 192
    mask = [step(4, i) for i in range(STEPS)]
    leak, face, crosses, verts = [], [], [], []
    for i in range(STEPS):
        m = mask[i]
        cross = jnp.where(inner_cross, step(2, i) * m * cross_next(m), 0.0)
        vert = jnp.where(inner_vert, step(3, i) * m * layer_next(m), 0.0)
        store = step(0, i)
        leak.append(store + cross + cross_prev(cross) + vert + layer_prev(vert))
        after = mask[i + 1] if i + 1 < STEPS else pltpu.roll(mask[0], SUBS - 1, 0)
        face.append(step(1, i) * m * after)
        crosses.append(cross)
        verts.append(vert)
        fields_ref[0, i] = cross
        fields_ref[1, i] = vert
        fields_ref[2, i] = m
        for s in range(2):
            head = step(5 + s, i)
            base = store * head
            base_ref[s, i] = base
            base_ref[2 + s, i] = base + coupled(cross, vert, head)
    coef, first, last, link = reduce_chain(leak, face[: STEPS - 1])
    leak1 = interleave(first, last)
    face1 = interleave(link, face[STEPS - 1])[: 2 * SUBS - 1]
    coef1, first1, last1, link1 = reduce_chain(leak1, face1)
    for k in range(3):
        for i in range(1, STEPS - 1):
            fields_ref[3 + k, i] = coef[k][i]
        for i in range(1, 2 * SUBS - 1):
            small_ref[k, i : i + 1] = coef1[k][i]
    one, zero = jnp.ones((1, 256), F32), jnp.zeros((1, 256), F32)
    basis = []
    for ends in ((one, zero), (zero, one)):
        basis.append(fill_chain(coef, None, *stack_ends(fill_chain(coef1, None, *ends))))
    for k in range(2):
        for i in range(STEPS):
            fields_ref[6 + k, i] = basis[k][i]
    gather_ref[0:1] = first1
    gather_ref[1:2] = last1
    gather_ref[2:3] = link1
    gather_ref[3:4] = both(lambda h: turned[1, h, 127:128, :] * turned[4, h, 127:128, :])
    gather_ref[4:5] = both(lambda h: turned[4, h, 0:1, :])
    for row, weight, move in ((5, crosses, cross_next), (9, verts, layer_next)):
        sums = [jnp.zeros((SUBS, 256), F32)] * 4
        for i in range(STEPS):
            moved = [move(basis[k][i]) for k in range(2)]
            for a in range(2):
                weighted = weight[i] * basis[a][i]
                for b in range(2):
                    sums[2 * a + b] = sums[2 * a + b] + weighted * moved[b]
        for k in range(4):
            gather_ref[row + k : row + k + 1] = column_sum(sums[k])


def load_coef(fields_ref, small_ref):
    coef = tuple([None] + [fields_ref[3 + k, i] for i in range(1, STEPS - 1)] + [None] for k in range(3))
    coef1 = tuple([None] + [small_ref[k, i : i + 1] for i in range(1, 2 * SUBS - 1)] + [None] for k in range(3))
    return coef, coef1


def local_solve(coef, coef1, rhs, first, last):
    part, ends_first, ends_last = reduce_source(coef[1], coef[2], rhs)
    part1, source_first, source_last = reduce_source(coef1[1], coef1[2], interleave(ends_first, ends_last))
    ends = stack_ends(fill_chain(coef1, part1, first, last))
    return fill_chain(coef, part, *ends), source_first, source_last


def source_kernel(fields_ref, small_ref, base_ref, own_ref, low_ref, high_ref, coefs_ref,
                  source_ref, inner_ref, out_ref, rain_scratch):
    rain_scratch[...] = own_ref[...] + low_ref[...] + high_ref[...]
    coef, coef1 = load_coef(fields_ref, small_ref)
    top = lax.broadcasted_iota(jnp.int32, (SUBS, 128), 1) < 64
    zero = jnp.zeros((1, 256), F32)
    none = jnp.zeros((SUBS, 128), F32)
    rows = []
    for s in range(2):
        rhs = []
        for i in range(STEPS):
            water = rain_scratch[step_rows(i), :]
            if s:
                water = pltpu.roll(water, 64, 1)
            water = jnp.concatenate([jnp.where(top, water, 0.0), none], axis=1) * fields_ref[2, i]
            source_ref[s, i] = base_ref[s, i] + water
            rhs.append(base_ref[2 + s, i] + water)
        inner, first, last = local_solve(coef, coef1, rhs, zero, zero)
        sums = [jnp.zeros((SUBS, 256), F32)] * 2
        for i in range(STEPS):
            inner_ref[s, i] = inner[i]
            later = source_ref[s, i] + coupled(fields_ref[0, i], fields_ref[1, i], inner[i])
            for k in range(2):
                sums[k] = sums[k] + fields_ref[6 + k, i] * later
        rows += [first, last, column_sum(sums[0]), column_sum(sums[1])]
    head = coefs_ref[0:13]
    block = jnp.concatenate([head] + rows + [jnp.zeros((3, 256), F32)], axis=0)
    for k in range(out_ref.shape[0]):
        for h in range(2):
            out_ref[k, ROWS * h : ROWS * h + ROWS] = block[:, 128 * h : 128 * h + 128]


def sweep_kernel(place_ref, gathered_ref, fields_ref, small_ref, source_ref, inner_ref,
                 head_ref, total_ref, ends_scratch, turned):
    devices = gathered_ref.shape[0] // (2 * ROWS)
    per = devices // SUBS

    def got(row, i):
        return both(lambda h: gathered_ref[pl.ds((2 * i + h) * ROWS + row, SUBS, stride=2 * per * ROWS), :])

    leak, face = [], []
    for i in range(per):
        leak += [got(0, i), got(1, i)]
        after = got(4, i + 1) if i + 1 < per else pltpu.roll(got(4, 0), SUBS - 1, 0)
        face += [got(2, i), got(3, i) * after]
    coef, first, last, link = reduce_chain(leak, face[: 2 * per - 1])
    leak1 = interleave(first, last)
    face1 = interleave(link, face[2 * per - 1])[: 2 * SUBS - 1]
    inv1, ratio1 = full_factor(leak1, face1)

    def across_devices(rhs):
        part, ends_first, ends_last = reduce_source(coef[1], coef[2], rhs)
        ends = full_solve(inv1, ratio1, interleave(ends_first, ends_last))
        return fill_chain(coef, part, *stack_ends(ends))

    cross_k = [[got(5 + k, i) for k in range(4)] for i in range(per)]
    vert_k = [[got(9 + k, i) for k in range(4)] for i in range(per)]
    for s in range(2):
        row = 13 + 4 * s
        ends = across_devices([got(row + a, i) for i in range(per) for a in range(2)])
        rhs = []
        for i in range(per):
            low, high = ends[2 * i], ends[2 * i + 1]
            later = [got(row + 2 + a, i) for a in range(2)]
            for k, ahead, back in ((cross_k[i], cross_next, cross_prev), (vert_k[i], layer_next, layer_prev)):
                low_ahead, high_ahead = ahead(low), ahead(high)
                later[0] = later[0] + k[0] * low_ahead + k[1] * high_ahead + back(k[0] * low + k[2] * high)
                later[1] = later[1] + k[2] * low_ahead + k[3] * high_ahead + back(k[1] * low + k[3] * high)
            rhs += later
        ends2 = across_devices(rhs)
        for i in range(per):
            for k, value in enumerate((ends[2 * i], ends[2 * i + 1], ends2[2 * i], ends2[2 * i + 1])):
                ends_scratch[4 * s + k, SUBS * i : SUBS * i + SUBS] = value
    coef, coef1 = load_coef(fields_ref, small_ref)
    place = place_ref[0]
    at = pl.ds((place % per) * SUBS + place // per, 1)
    for s in range(2):
        low1, high1, low2, high2 = [ends_scratch[4 * s + k, at, :] for k in range(4)]
        rhs = []
        for i in range(STEPS):
            head = inner_ref[s, i] + fields_ref[6, i] * low1 + fields_ref[7, i] * high1
            rhs.append(source_ref[s, i] + coupled(fields_ref[0, i], fields_ref[1, i], head))
        solved, _, _ = local_solve(coef, coef1, rhs, low2, high2)
        for i in range(STEPS):
            for h in range(2):
                turned[s, h, step_rows(i), :] = solved[i][:, 128 * h : 128 * h + 128]
    for h in range(2):
        lanes = [turned[s, h].T for s in range(2)]
        for s in range(2):
            head_ref[s, 2 * h : 2 * h + 2] = lanes[s].reshape(2, 64, 128)
        total_ref[2 * h : 2 * h + 2] = (lanes[0] + lanes[1]).reshape(2, 64, 128)


VMEM = pl.BlockSpec(memory_space=pltpu.VMEM)
SMEM = pl.BlockSpec(memory_space=pltpu.SMEM)


def kernel_call(body, name, specs, outs, scratch, flops):
    return pl.pallas_call(
        body,
        name=name,
        in_specs=specs,
        out_specs=[VMEM] * len(outs),
        out_shape=[jax.ShapeDtypeStruct(shape, F32) for shape in outs],
        scratch_shapes=[pltpu.VMEM(shape, F32) for shape in scratch],
        compiler_params=pltpu.CompilerParams(vmem_limit_bytes=48 * 2**20),
        cost_estimate=pl.CostEstimate(flops=flops, bytes_accessed=2 * 2**20, transcendentals=0),
    )


def on_device(
    head_prev,
    storage,
    cond_flow,
    cond_cross,
    cond_vert,
    active,
    hru_cells,
    hru_area,
    hru_land,
    hru_bmp,
    rain,
    perc_table,
    hru_live,
):
    slots = hru_land.shape[0]
    devices = lax.axis_size("flow")
    tile = (128, 128)
    blocks = [(4, slots), (4, slots), (1, slots), (2, slots), (1, slots), (8, 16)]
    before, own, after = pl.pallas_call(
        scatter_kernel,
        name="scatter",
        grid=(1,),
        in_specs=[pl.BlockSpec(shape, lambda i: (0, 0)) for shape in blocks] + [SMEM],
        out_specs=[pl.BlockSpec(tile, lambda i: (0, 0))] * 3,
        out_shape=[jax.ShapeDtypeStruct(tile, F32)] * 3,
        scratch_shapes=[pltpu.VMEM((4, 4, slots), F32), pltpu.VMEM((3,) + tile, F32)],
        compiler_params=pltpu.CompilerParams(vmem_limit_bytes=60 * 2**20),
        cost_estimate=pl.CostEstimate(flops=4 * 10**9, bytes_accessed=2 * 2**20, transcendentals=0),
    )(
        hru_cells.T, hru_area.T, hru_land.reshape(1, slots), hru_bmp, rain.reshape(1, slots), perc_table.T, hru_live
    )
    high = lax.ppermute(before, "flow", [(i + 1, i) for i in range(devices - 1)])
    low = lax.ppermute(after, "flow", [(i, i + 1) for i in range(devices - 1)])
    fields, small, base, coefs = kernel_call(
        coefficient_kernel,
        "coefficients",
        [VMEM] * 6,
        [(8, STEPS, SUBS, 256), (3, 2 * SUBS, 256), (4, STEPS, SUBS, 256), (16, 256)],
        [(7, 2, 128, 128)],
        4 * 10**9,
    )(head_prev, storage, cond_flow, cond_cross, cond_vert, active)
    source, inner, block = kernel_call(
        source_kernel,
        "sources",
        [VMEM] * 7,
        [(2, STEPS, SUBS, 256), (2, STEPS, SUBS, 256), (devices, 2 * ROWS, 128)],
        [tile],
        10**9,
    )(fields, small, base, own, low, high, coefs)
    place = lax.axis_index("flow").astype(jnp.int32).reshape(1)
    block, place = lax.optimization_barrier((block, place))
    gathered = lax.all_to_all(block, "flow", split_axis=0, concat_axis=0, tiled=True)
    head, total = kernel_call(
        sweep_kernel,
        "sweeps",
        [SMEM] + [VMEM] * 5,
        [head_prev.shape, storage.shape],
        [(8, devices, 256), (2, 2, 128, 128)],
        10**9,
    )(place, gathered.reshape(devices * 2 * ROWS, 128), fields, small, source, inner)
    lanes = lax.axis_size("lane")
    total = total + lax.ppermute(total, "lane", [(i, i ^ 1) for i in range(lanes)])
    whole = total
    for k in range(2, lanes, 2):
        whole = whole + lax.ppermute(total, "lane", [(i, (i + k) % lanes) for i in range(lanes)])
    anomaly = head - whole[None] / (2 * lanes)
    return head, anomaly


def solution(mesh):
    return jax.shard_map(
        on_device,
        mesh=mesh,
        in_specs=(
            P("lane", None, None, "flow"),
            P(None, None, "flow"),
            P(None, None, "flow"),
            P(None, None, "flow"),
            P(None, None, "flow"),
            P(None, None, "flow"),
            P("flow", None),
            P("flow", None),
            P("flow"),
            P("lane", "flow"),
            P("flow"),
            P(),
            P("flow"),
        ),
        out_specs=(P("lane", None, None, "flow"), P("lane", None, None, "flow")),
        check_vma=False,
    )
```

```python
import functools

import jax
import jax.numpy as jnp
from jax import lax
from jax.experimental import pallas as pl
from jax.experimental.pallas import tpu as pltpu
from jax.sharding import PartitionSpec as P

STEPS = 16
SUBS = 8
ROWS = 24
F32 = jnp.float32
BF16 = jnp.bfloat16


def halves(fn, a):
    return jnp.concatenate([fn(a[:, :128]), fn(a[:, 128:])], axis=1)


def cross_next(a):
    return halves(lambda h: pltpu.roll(h, 127, 1), a)


def cross_prev(a):
    return halves(lambda h: pltpu.roll(h, 1, 1), a)


def layer_rolls(a):
    lo = lax.broadcasted_iota(jnp.int32, (a.shape[0], 128), 1) < 64
    return lo, pltpu.roll(a[:, :128], 64, 1), pltpu.roll(a[:, 128:], 64, 1)


def layer_next(a):
    lo, r0, r1 = layer_rolls(a)
    return jnp.concatenate([jnp.where(lo, r0, r1), jnp.where(lo, r1, r0)], axis=1)


def layer_prev(a):
    lo, r0, r1 = layer_rolls(a)
    return jnp.concatenate([jnp.where(lo, r1, r0), jnp.where(lo, r0, r1)], axis=1)


def coupled(cross, vert, head):
    out = cross * cross_next(head) + cross_prev(cross * head)
    return out + vert * layer_next(head) + layer_prev(vert * head)


def reduce_chain(leak, face):
    n = len(leak)
    first, link, shunt = leak[0], face[0], leak[1]
    inv, ratio, share = [None] * n, [None] * n, [None] * n
    for i in range(1, n - 1):
        inv[i] = 1.0 / (face[i] + (shunt + link))
        ratio[i] = face[i] * inv[i]
        share[i] = link * inv[i]
        first = first + shunt * share[i]
        shunt = leak[i + 1] + shunt * ratio[i]
        link = link * ratio[i]
    return (inv, ratio, share), first, shunt, link


def reduce_source(ratio, share, rhs):
    n = len(rhs)
    first = rhs[0]
    part = [None] * n
    part[1] = rhs[1]
    for i in range(1, n - 1):
        first = first + share[i] * part[i]
        part[i + 1] = rhs[i + 1] + ratio[i] * part[i]
    return part, first, part[n - 1]


def fill_chain(coef, part, first, last):
    inv, ratio, share = coef
    n = len(ratio)
    out = [None] * n
    out[0], out[n - 1] = first, last
    for i in range(n - 2, 0, -1):
        value = share[i] * first + ratio[i] * out[i + 1]
        out[i] = value if part is None else value + inv[i] * part[i]
    return out


def full_factor(leak, face):
    n = len(leak)
    shunt = leak[0]
    inv, ratio = [None] * n, [None] * n
    for i in range(n - 1):
        inv[i] = 1.0 / (face[i] + shunt)
        ratio[i] = face[i] * inv[i]
        shunt = leak[i + 1] + shunt * ratio[i]
    inv[n - 1] = 1.0 / shunt
    return inv, ratio


def full_solve(inv, ratio, rhs):
    n = len(rhs)
    part = [rhs[0]]
    for i in range(n - 1):
        part.append(rhs[i + 1] + ratio[i] * part[i])
    out = [None] * n
    out[n - 1] = inv[n - 1] * part[n - 1]
    for i in range(n - 2, -1, -1):
        out[i] = inv[i] * part[i] + ratio[i] * out[i + 1]
    return out


def to_rows(a):
    return [a[k : k + 1] for k in range(SUBS)]


def interleave(a, b):
    return [x for pair in zip(to_rows(a), to_rows(b)) for x in pair]


def stack_ends(nodes):
    return jnp.concatenate(nodes[0::2], axis=0), jnp.concatenate(nodes[1::2], axis=0)


def column_sum(a):
    return jnp.sum(a, axis=0, keepdims=True)


def both(fn):
    return jnp.concatenate([fn(0), fn(1)], axis=1)


def step_rows(i):
    return pl.ds(i, SUBS, stride=STEPS)


def scatter_kernel(cells_ref, area_ref, land_ref, bmp_ref, rain_ref, table_ref, live_ref,
                   before_ref, own_ref, after_ref, amount_ref, window_ref):
    slots = land_ref.shape[1]
    land = land_ref[...]
    rates = jnp.zeros((8, slots), F32)
    for use in range(table_ref.shape[1]):
        rates = jnp.where(land == use, table_ref[:, use : use + 1], rates)
    bmp = bmp_ref[...]
    chosen = jnp.zeros(bmp.shape, F32)
    for code in range(table_ref.shape[0]):
        chosen = jnp.where(bmp == code, rates[code : code + 1], chosen)
    alive = lax.broadcasted_iota(jnp.int32, (1, slots), 1) < live_ref[0]
    perc = jnp.where(alive, rain_ref[...] * chosen, 0.0)
    for q in range(4):
        amount = perc * area_ref[q : q + 1, :]
        high = amount.astype(BF16).astype(F32)
        amount_ref[q, 0:2, :] = high
        amount_ref[q, 2:4, :] = amount - high
    column = lax.broadcasted_iota(jnp.int32, (256, slots), 0).astype(F32).astype(BF16)
    line = lax.broadcasted_iota(jnp.int32, (96, slots), 0).astype(F32).astype(BF16)
    one, zero = jnp.ones((), BF16), jnp.zeros((), BF16)
    total = None
    for q in range(4):
        cell = cells_ref[q : q + 1, :]
        columns = jnp.where(column == (cell & 255).astype(F32).astype(BF16), one, zero)
        hit = line == (cell >> 8).astype(F32).astype(BF16)
        put = [jnp.where(hit, amount_ref[q, k : k + 1, :].astype(BF16), zero) for k in (0, 2, 1, 3)]
        product = lax.dot_general(
            jnp.concatenate(put, axis=0), columns, (((1,), (1,)), ((), ())), preferred_element_type=F32
        )
        total = product if total is None else total + product
    for s in range(2):
        summed = total[192 * s : 192 * s + 96] + total[192 * s + 96 : 192 * s + 192]
        for k in range(3):
            for odd in range(2):
                window_ref[k, pl.ds(64 * s + odd, 32, stride=2), :] = summed[
                    32 * k : 32 * k + 32, 128 * odd : 128 * odd + 128
                ]
    for k, ref in enumerate((before_ref, own_ref, after_ref)):
        ref[...] = window_ref[k].T


def coefficient_kernel(head_ref, storage_ref, flow_ref, cross_ref, vert_ref, active_ref,
                       fields_ref, small_ref, base_ref, gather_ref, turned):
    def turn(slot, part):
        for h in range(2):
            turned[slot, h] = part(h).T

    for slot, ref in enumerate((storage_ref, flow_ref, cross_ref, vert_ref)):
        turn(slot, lambda h: ref[2 * h : 2 * h + 2].reshape(128, 128))
    turn(4, lambda h: active_ref[2 * h : 2 * h + 2].reshape(128, 128).astype(F32))
    for s in range(2):
        turn(5 + s, lambda h: head_ref[s, 2 * h : 2 * h + 2].reshape(128, 128))

    def step(slot, i):
        return both(lambda h: turned[slot, h, step_rows(i), :])

    lane = lax.broadcasted_iota(jnp.int32, (SUBS, 256), 1)
    inner_cross = lane % 64 != 63
    inner_vert = lane < 192
    mask = [step(4, i) for i in range(STEPS)]
    leak, face, crosses, verts = [], [], [], []
    for i in range(STEPS):
        m = mask[i]
        cross = jnp.where(inner_cross, step(2, i) * m * cross_next(m), 0.0)
        vert = jnp.where(inner_vert, step(3, i) * m * layer_next(m), 0.0)
        store = step(0, i)
        leak.append(store + cross + cross_prev(cross) + vert + layer_prev(vert))
        after = mask[i + 1] if i + 1 < STEPS else pltpu.roll(mask[0], SUBS - 1, 0)
        face.append(step(1, i) * m * after)
        crosses.append(cross)
        verts.append(vert)
        fields_ref[0, i] = cross
        fields_ref[1, i] = vert
        fields_ref[2, i] = m
        for s in range(2):
            head = step(5 + s, i)
            base = store * head
            base_ref[s, i] = base
            base_ref[2 + s, i] = base + coupled(cross, vert, head)
    coef, first, last, link = reduce_chain(leak, face[: STEPS - 1])
    leak1 = interleave(first, last)
    face1 = interleave(link, face[STEPS - 1])[: 2 * SUBS - 1]
    coef1, first1, last1, link1 = reduce_chain(leak1, face1)
    for k in range(3):
        for i in range(1, STEPS - 1):
            fields_ref[3 + k, i] = coef[k][i]
        for i in range(1, 2 * SUBS - 1):
            small_ref[k, i : i + 1] = coef1[k][i]
    one, zero = jnp.ones((1, 256), F32), jnp.zeros((1, 256), F32)
    basis = []
    for ends in ((one, zero), (zero, one)):
        basis.append(fill_chain(coef, None, *stack_ends(fill_chain(coef1, None, *ends))))
    for k in range(2):
        for i in range(STEPS):
            fields_ref[6 + k, i] = basis[k][i]
    gather_ref[0:1] = first1
    gather_ref[1:2] = last1
    gather_ref[2:3] = link1
    gather_ref[3:4] = both(lambda h: turned[1, h, 127:128, :] * turned[4, h, 127:128, :])
    gather_ref[4:5] = both(lambda h: turned[4, h, 0:1, :])
    for row, weight, move in ((5, crosses, cross_next), (9, verts, layer_next)):
        sums = [jnp.zeros((SUBS, 256), F32)] * 4
        for i in range(STEPS):
            moved = [move(basis[k][i]) for k in range(2)]
            for a in range(2):
                weighted = weight[i] * basis[a][i]
                for b in range(2):
                    sums[2 * a + b] = sums[2 * a + b] + weighted * moved[b]
        for k in range(4):
            gather_ref[row + k : row + k + 1] = column_sum(sums[k])


def load_coef(fields_ref, small_ref):
    coef = tuple([None] + [fields_ref[3 + k, i] for i in range(1, STEPS - 1)] + [None] for k in range(3))
    coef1 = tuple([None] + [small_ref[k, i : i + 1] for i in range(1, 2 * SUBS - 1)] + [None] for k in range(3))
    return coef, coef1


def local_solve(coef, coef1, rhs, first, last):
    part, ends_first, ends_last = reduce_source(coef[1], coef[2], rhs)
    part1, source_first, source_last = reduce_source(coef1[1], coef1[2], interleave(ends_first, ends_last))
    ends = stack_ends(fill_chain(coef1, part1, first, last))
    return fill_chain(coef, part, *ends), source_first, source_last


def source_kernel(fields_ref, small_ref, base_ref, own_ref, low_ref, high_ref, coefs_ref,
                  source_ref, inner_ref, out_ref, rain_scratch):
    rain_scratch[...] = own_ref[...] + low_ref[...] + high_ref[...]
    coef, coef1 = load_coef(fields_ref, small_ref)
    top = lax.broadcasted_iota(jnp.int32, (SUBS, 128), 1) < 64
    zero = jnp.zeros((1, 256), F32)
    none = jnp.zeros((SUBS, 128), F32)
    rows = []
    for s in range(2):
        rhs = []
        for i in range(STEPS):
            water = rain_scratch[step_rows(i), :]
            if s:
                water = pltpu.roll(water, 64, 1)
            water = jnp.concatenate([jnp.where(top, water, 0.0), none], axis=1) * fields_ref[2, i]
            source_ref[s, i] = base_ref[s, i] + water
            rhs.append(base_ref[2 + s, i] + water)
        inner, first, last = local_solve(coef, coef1, rhs, zero, zero)
        sums = [jnp.zeros((SUBS, 256), F32)] * 2
        for i in range(STEPS):
            inner_ref[s, i] = inner[i]
            later = source_ref[s, i] + coupled(fields_ref[0, i], fields_ref[1, i], inner[i])
            for k in range(2):
                sums[k] = sums[k] + fields_ref[6 + k, i] * later
        rows += [first, last, column_sum(sums[0]), column_sum(sums[1])]
    put_block(out_ref, [coefs_ref[k : k + 1] for k in range(13)] + rows)


def put_block(ref, rows):
    for k in range(ROWS):
        row = rows[k] if k < len(rows) else jnp.zeros((1, 256), F32)
        for h in range(2):
            ref[ROWS * h + k : ROWS * h + k + 1] = row[:, 128 * h : 128 * h + 128]


def coupled_ends(got, later, low, high):
    for row, ahead, back in ((5, cross_next, cross_prev), (9, layer_next, layer_prev)):
        k = [got(row + m) for m in range(4)]
        low_ahead, high_ahead = ahead(low), ahead(high)
        later = (
            later[0] + k[0] * low_ahead + k[1] * high_ahead + back(k[0] * low + k[2] * high),
            later[1] + k[2] * low_ahead + k[3] * high_ahead + back(k[1] * low + k[3] * high),
        )
    return later


def member(blocks_ref, p):
    return lambda row: both(lambda h: blocks_ref[p, ROWS * h + row : ROWS * h + row + 1, :])


def group_later(blocks_ref, s, nodes):
    out = []
    for p in range(blocks_ref.shape[0]):
        got = member(blocks_ref, p)
        out += coupled_ends(got, (got(15 + 4 * s), got(16 + 4 * s)), nodes[2 * p], nodes[2 * p + 1])
    return out


def group_kernel(place_ref, own_ref, from1_ref, from2_ref, from3_ref, blocks_ref, saved_ref, out_ref, block):
    per = blocks_ref.shape[0]
    place = lax.rem(place_ref[0], per)
    for k, ref in enumerate((own_ref, from1_ref, from2_ref, from3_ref)):
        blocks_ref[lax.rem(place + per - k, per)] = ref[...]
    got = [member(blocks_ref, p) for p in range(per)]
    leak, face = [], []
    for p in range(per):
        leak += [got[p](0), got[p](1)]
        face.append(got[p](2))
        if p + 1 < per:
            face.append(got[p](3) * got[p + 1](4))
    coef, first, last, link = reduce_chain(leak, face)
    nodes = 2 * per
    one, zero = jnp.ones((1, 256), F32), jnp.zeros((1, 256), F32)
    basis = [fill_chain(coef, None, one, zero), fill_chain(coef, None, zero, one)]
    for k in range(3):
        for i in range(1, nodes - 1):
            saved_ref[nodes * k + i : nodes * k + i + 1] = coef[k][i]
    rows = [first, last, link, got[per - 1](3), got[0](4)]
    for row, move in ((5, cross_next), (9, layer_next)):
        sums = [zero] * 4
        for p in range(per):
            moved = [[move(basis[b][2 * p + e]) for e in range(2)] for b in range(2)]
            k = [got[p](row + m) for m in range(4)]
            for b in range(2):
                ends = [k[2 * e] * moved[b][0] + k[2 * e + 1] * moved[b][1] for e in range(2)]
                for a in range(2):
                    sums[2 * a + b] = sums[2 * a + b] + basis[a][2 * p] * ends[0] + basis[a][2 * p + 1] * ends[1]
        rows += sums
    for s in range(2):
        rhs = [got[p](13 + 4 * s + e) for p in range(per) for e in range(2)]
        part, source_first, source_last = reduce_source(coef[1], coef[2], rhs)
        inner = fill_chain(coef, part, zero, zero)
        _, later_first, later_last = reduce_source(coef[1], coef[2], group_later(blocks_ref, s, inner))
        rows += [source_first, source_last, later_first, later_last]
        for i in range(nodes):
            saved_ref[nodes * (5 + s) + i : nodes * (5 + s) + i + 1] = inner[i]
            saved_ref[nodes * (3 + s) + i : nodes * (3 + s) + i + 1] = basis[s][i]
    put_block(block, rows)
    for k in range(out_ref.shape[0]):
        out_ref[k] = block[...]


def sweep_kernel(place_ref, gathered_ref, blocks_ref, saved_ref, fields_ref, small_ref, source_ref, inner_ref,
                 head_ref, total_ref, ends_scratch, turned):
    per = blocks_ref.shape[0]
    groups = gathered_ref.shape[0] // (2 * ROWS)
    place = place_ref[0]

    def got(row):
        return both(lambda h: gathered_ref[pl.ds(ROWS * h + row, groups, stride=2 * ROWS), :])

    face = got(3) * pltpu.roll(got(4), groups - 1, 0)
    inv, ratio = full_factor(interleave(got(0), got(1)), interleave(got(2), face)[: 2 * groups - 1])
    nodes = 2 * per
    saved = [[saved_ref[nodes * k + i : nodes * k + i + 1] for i in range(nodes)] for k in range(7)]
    at = pl.ds(place // per, 1)
    pick = pl.ds(lax.rem(place, per), 1)
    ends = []
    for s in range(2):
        row = 13 + 4 * s
        low, high = stack_ends(full_solve(inv, ratio, interleave(got(row), got(row + 1))))
        later = coupled_ends(got, (got(row + 2), got(row + 3)), low, high)
        low2, high2 = stack_ends(full_solve(inv, ratio, interleave(*later)))
        for k, value in enumerate((low, high, low2, high2)):
            ends_scratch[k] = value
        low, high, low2, high2 = [ends_scratch[k, at, :] for k in range(4)]
        first = [saved[5 + s][i] + saved[3][i] * low + saved[4][i] * high for i in range(nodes)]
        part, _, _ = reduce_source(saved[1], saved[2], group_later(blocks_ref, s, first))
        second = fill_chain(tuple(saved[:3]), part, low2, high2)
        for k, values in enumerate((first[0::2], first[1::2], second[0::2], second[1::2])):
            for p in range(per):
                ends_scratch[k, p : p + 1] = values[p]
        ends.append([ends_scratch[k, pick, :] for k in range(4)])
    coef, coef1 = load_coef(fields_ref, small_ref)
    for s in range(2):
        low1, high1, low2, high2 = ends[s]
        rhs = []
        for i in range(STEPS):
            head = inner_ref[s, i] + fields_ref[6, i] * low1 + fields_ref[7, i] * high1
            rhs.append(source_ref[s, i] + coupled(fields_ref[0, i], fields_ref[1, i], head))
        solved, _, _ = local_solve(coef, coef1, rhs, low2, high2)
        for i in range(STEPS):
            for h in range(2):
                turned[s, h, step_rows(i), :] = solved[i][:, 128 * h : 128 * h + 128]
    for h in range(2):
        lanes = [turned[s, h].T for s in range(2)]
        for s in range(2):
            head_ref[s, 2 * h : 2 * h + 2] = lanes[s].reshape(2, 64, 128)
        total_ref[2 * h : 2 * h + 2] = (lanes[0] + lanes[1]).reshape(2, 64, 128)


VMEM = pl.BlockSpec(memory_space=pltpu.VMEM)
SMEM = pl.BlockSpec(memory_space=pltpu.SMEM)


def kernel_call(body, name, specs, outs, scratch, flops):
    return pl.pallas_call(
        body,
        name=name,
        in_specs=specs,
        out_specs=[VMEM] * len(outs),
        out_shape=[jax.ShapeDtypeStruct(shape, F32) for shape in outs],
        scratch_shapes=[pltpu.VMEM(shape, F32) for shape in scratch],
        compiler_params=pltpu.CompilerParams(vmem_limit_bytes=48 * 2**20),
        cost_estimate=pl.CostEstimate(flops=flops, bytes_accessed=2 * 2**20, transcendentals=0),
    )


def on_device(
    head_prev,
    storage,
    cond_flow,
    cond_cross,
    cond_vert,
    active,
    hru_cells,
    hru_area,
    hru_land,
    hru_bmp,
    rain,
    perc_table,
    hru_live,
):
    slots = hru_land.shape[0]
    devices = lax.axis_size("flow")
    tile = (128, 128)
    blocks = [(4, slots), (4, slots), (1, slots), (2, slots), (1, slots), (8, 16)]
    before, own, after = pl.pallas_call(
        scatter_kernel,
        name="scatter",
        grid=(1,),
        in_specs=[pl.BlockSpec(shape, lambda i: (0, 0)) for shape in blocks] + [SMEM],
        out_specs=[pl.BlockSpec(tile, lambda i: (0, 0))] * 3,
        out_shape=[jax.ShapeDtypeStruct(tile, F32)] * 3,
        scratch_shapes=[pltpu.VMEM((4, 4, slots), F32), pltpu.VMEM((3,) + tile, F32)],
        compiler_params=pltpu.CompilerParams(vmem_limit_bytes=60 * 2**20),
        cost_estimate=pl.CostEstimate(flops=4 * 10**9, bytes_accessed=2 * 2**20, transcendentals=0),
    )(
        hru_cells.T, hru_area.T, hru_land.reshape(1, slots), hru_bmp, rain.reshape(1, slots), perc_table.T, hru_live
    )
    high = lax.ppermute(before, "flow", [(i + 1, i) for i in range(devices - 1)])
    low = lax.ppermute(after, "flow", [(i, i + 1) for i in range(devices - 1)])
    fields, small, base, coefs = kernel_call(
        coefficient_kernel,
        "coefficients",
        [VMEM] * 6,
        [(8, STEPS, SUBS, 256), (3, 2 * SUBS, 256), (4, STEPS, SUBS, 256), (16, 256)],
        [(7, 2, 128, 128)],
        4 * 10**9,
    )(head_prev, storage, cond_flow, cond_cross, cond_vert, active)
    source, inner, block = kernel_call(
        source_kernel,
        "sources",
        [VMEM] * 7,
        [(2, STEPS, SUBS, 256), (2, STEPS, SUBS, 256), (2 * ROWS, 128)],
        [tile],
        10**9,
    )(fields, small, base, own, low, high, coefs)
    place = lax.axis_index("flow").astype(jnp.int32).reshape(1)
    per = devices // SUBS
    around = [
        lax.ppermute(block, "flow", [(i, i - i % per + (i + k) % per) for i in range(devices)]) for k in range(1, per)
    ]
    blocks, saved, block = kernel_call(
        group_kernel,
        "groups",
        [SMEM] + [VMEM] * per,
        [(per, 2 * ROWS, 128), (14 * per, 256), (SUBS, 2 * ROWS, 128)],
        [(2 * ROWS, 128)],
        10**9,
    )(place, block, *around)
    same = [[i + per * k for k in range(SUBS)] for i in range(per)]
    gathered = lax.all_to_all(block, "flow", split_axis=0, concat_axis=0, axis_index_groups=same, tiled=True)
    head, total = kernel_call(
        sweep_kernel,
        "sweeps",
        [SMEM] + [VMEM] * 7,
        [head_prev.shape, storage.shape],
        [(4, SUBS, 256), (2, 2, 128, 128)],
        10**9,
    )(place, gathered.reshape(SUBS * 2 * ROWS, 128), blocks, saved, fields, small, source, inner)
    lanes = lax.axis_size("lane")
    total = total + lax.ppermute(total, "lane", [(i, i ^ 1) for i in range(lanes)])
    whole = total
    for k in range(2, lanes, 2):
        whole = whole + lax.ppermute(total, "lane", [(i, (i + k) % lanes) for i in range(lanes)])
    anomaly = head - whole[None] / (2 * lanes)
    return head, anomaly


def solution(mesh):
    return jax.shard_map(
        on_device,
        mesh=mesh,
        in_specs=(
            P("lane", None, None, "flow"),
            P(None, None, "flow"),
            P(None, None, "flow"),
            P(None, None, "flow"),
            P(None, None, "flow"),
            P(None, None, "flow"),
            P("flow", None),
            P("flow", None),
            P("flow"),
            P("lane", "flow"),
            P("flow"),
            P(),
            P("flow"),
        ),
        out_specs=(P("lane", None, None, "flow"), P("lane", None, None, "flow")),
        check_vma=False,
    )
```

```python
import functools

import jax
import jax.numpy as jnp
from jax import lax
from jax.experimental import pallas as pl
from jax.experimental.pallas import tpu as pltpu
from jax.sharding import PartitionSpec as P

STEPS = 16
SUBS = 8
ROWS = 24
F32 = jnp.float32
BF16 = jnp.bfloat16


def halves(fn, a):
    return jnp.concatenate([fn(a[:, :128]), fn(a[:, 128:])], axis=1)


def cross_next(a):
    return halves(lambda h: pltpu.roll(h, 127, 1), a)


def cross_prev(a):
    return halves(lambda h: pltpu.roll(h, 1, 1), a)


def layer_rolls(a):
    lo = lax.broadcasted_iota(jnp.int32, (a.shape[0], 128), 1) < 64
    return lo, pltpu.roll(a[:, :128], 64, 1), pltpu.roll(a[:, 128:], 64, 1)


def layer_next(a):
    lo, r0, r1 = layer_rolls(a)
    return jnp.concatenate([jnp.where(lo, r0, r1), jnp.where(lo, r1, r0)], axis=1)


def layer_prev(a):
    lo, r0, r1 = layer_rolls(a)
    return jnp.concatenate([jnp.where(lo, r1, r0), jnp.where(lo, r0, r1)], axis=1)


def coupled(cross, vert, head):
    out = cross * cross_next(head) + cross_prev(cross * head)
    return out + vert * layer_next(head) + layer_prev(vert * head)


def reduce_chain(leak, face):
    n = len(leak)
    first, link, shunt = leak[0], face[0], leak[1]
    inv, ratio, share = [None] * n, [None] * n, [None] * n
    for i in range(1, n - 1):
        inv[i] = 1.0 / (face[i] + (shunt + link))
        ratio[i] = face[i] * inv[i]
        share[i] = link * inv[i]
        first = first + shunt * share[i]
        shunt = leak[i + 1] + shunt * ratio[i]
        link = link * ratio[i]
    return (inv, ratio, share), first, shunt, link


def reduce_source(ratio, share, rhs):
    n = len(rhs)
    first = rhs[0]
    part = [None] * n
    part[1] = rhs[1]
    for i in range(1, n - 1):
        first = first + share[i] * part[i]
        part[i + 1] = rhs[i + 1] + ratio[i] * part[i]
    return part, first, part[n - 1]


def fill_chain(coef, part, first, last):
    inv, ratio, share = coef
    n = len(ratio)
    out = [None] * n
    out[0], out[n - 1] = first, last
    for i in range(n - 2, 0, -1):
        value = share[i] * first + ratio[i] * out[i + 1]
        out[i] = value if part is None else value + inv[i] * part[i]
    return out


def full_factor(leak, face):
    n = len(leak)
    shunt = leak[0]
    inv, ratio = [None] * n, [None] * n
    for i in range(n - 1):
        inv[i] = 1.0 / (face[i] + shunt)
        ratio[i] = face[i] * inv[i]
        shunt = leak[i + 1] + shunt * ratio[i]
    inv[n - 1] = 1.0 / shunt
    return inv, ratio


def full_solve(inv, ratio, rhs):
    n = len(rhs)
    part = [rhs[0]]
    for i in range(n - 1):
        part.append(rhs[i + 1] + ratio[i] * part[i])
    out = [None] * n
    out[n - 1] = inv[n - 1] * part[n - 1]
    for i in range(n - 2, -1, -1):
        out[i] = inv[i] * part[i] + ratio[i] * out[i + 1]
    return out


def to_rows(a):
    return [a[k : k + 1] for k in range(SUBS)]


def interleave(a, b):
    return [x for pair in zip(to_rows(a), to_rows(b)) for x in pair]


def stack_ends(nodes):
    return jnp.concatenate(nodes[0::2], axis=0), jnp.concatenate(nodes[1::2], axis=0)


def column_sum(a):
    return jnp.sum(a, axis=0, keepdims=True)


def both(fn):
    return jnp.concatenate([fn(0), fn(1)], axis=1)


def step_rows(i):
    return pl.ds(i, SUBS, stride=STEPS)


def scatter_kernel(cells_ref, area_ref, land_ref, bmp_ref, rain_ref, table_ref, live_ref,
                   before_ref, own_ref, after_ref, amount_ref, window_ref):
    slots = land_ref.shape[1]
    land = land_ref[...]
    rates = jnp.zeros((8, slots), F32)
    for use in range(table_ref.shape[1]):
        rates = jnp.where(land == use, table_ref[:, use : use + 1], rates)
    bmp = bmp_ref[...]
    chosen = jnp.zeros(bmp.shape, F32)
    for code in range(table_ref.shape[0]):
        chosen = jnp.where(bmp == code, rates[code : code + 1], chosen)
    alive = lax.broadcasted_iota(jnp.int32, (1, slots), 1) < live_ref[0]
    perc = jnp.where(alive, rain_ref[...] * chosen, 0.0)
    for q in range(4):
        amount = perc * area_ref[q : q + 1, :]
        high = amount.astype(BF16).astype(F32)
        amount_ref[q, 0:2, :] = high
        amount_ref[q, 2:4, :] = amount - high
    column = lax.broadcasted_iota(jnp.int32, (256, slots), 0).astype(F32).astype(BF16)
    line = lax.broadcasted_iota(jnp.int32, (96, slots), 0).astype(F32).astype(BF16)
    one, zero = jnp.ones((), BF16), jnp.zeros((), BF16)
    total = None
    for q in range(4):
        cell = cells_ref[q : q + 1, :]
        columns = jnp.where(column == (cell & 255).astype(F32).astype(BF16), one, zero)
        hit = line == (cell >> 8).astype(F32).astype(BF16)
        put = [jnp.where(hit, amount_ref[q, k : k + 1, :].astype(BF16), zero) for k in (0, 2, 1, 3)]
        product = lax.dot_general(
            jnp.concatenate(put, axis=0), columns, (((1,), (1,)), ((), ())), preferred_element_type=F32
        )
        total = product if total is None else total + product
    for s in range(2):
        summed = total[192 * s : 192 * s + 96] + total[192 * s + 96 : 192 * s + 192]
        for k in range(3):
            for odd in range(2):
                window_ref[k, pl.ds(64 * s + odd, 32, stride=2), :] = summed[
                    32 * k : 32 * k + 32, 128 * odd : 128 * odd + 128
                ]
    for k, ref in enumerate((before_ref, own_ref, after_ref)):
        ref[...] = window_ref[k].T


def coefficient_kernel(head_ref, storage_ref, flow_ref, cross_ref, vert_ref, active_ref,
                       fields_ref, small_ref, base_ref, gather_ref, turned):
    def turn(slot, part):
        for h in range(2):
            turned[slot, h] = part(h).T

    for slot, ref in enumerate((storage_ref, flow_ref, cross_ref, vert_ref)):
        turn(slot, lambda h: ref[2 * h : 2 * h + 2].reshape(128, 128))
    turn(4, lambda h: active_ref[2 * h : 2 * h + 2].reshape(128, 128).astype(F32))
    for s in range(2):
        turn(5 + s, lambda h: head_ref[s, 2 * h : 2 * h + 2].reshape(128, 128))

    def step(slot, i):
        return both(lambda h: turned[slot, h, step_rows(i), :])

    lane = lax.broadcasted_iota(jnp.int32, (SUBS, 256), 1)
    inner_cross = lane % 64 != 63
    inner_vert = lane < 192
    mask = [step(4, i) for i in range(STEPS)]
    leak, face, crosses, verts = [], [], [], []
    for i in range(STEPS):
        m = mask[i]
        cross = jnp.where(inner_cross, step(2, i) * m * cross_next(m), 0.0)
        vert = jnp.where(inner_vert, step(3, i) * m * layer_next(m), 0.0)
        store = step(0, i)
        leak.append(store + cross + cross_prev(cross) + vert + layer_prev(vert))
        after = mask[i + 1] if i + 1 < STEPS else pltpu.roll(mask[0], SUBS - 1, 0)
        face.append(step(1, i) * m * after)
        crosses.append(cross)
        verts.append(vert)
        fields_ref[0, i] = cross
        fields_ref[1, i] = vert
        fields_ref[2, i] = m
        for s in range(2):
            head = step(5 + s, i)
            base = store * head
            base_ref[s, i] = base
            base_ref[2 + s, i] = base + coupled(cross, vert, head)
    coef, first, last, link = reduce_chain(leak, face[: STEPS - 1])
    leak1 = interleave(first, last)
    face1 = interleave(link, face[STEPS - 1])[: 2 * SUBS - 1]
    coef1, first1, last1, link1 = reduce_chain(leak1, face1)
    for k in range(3):
        for i in range(1, STEPS - 1):
            fields_ref[3 + k, i] = coef[k][i]
        for i in range(1, 2 * SUBS - 1):
            small_ref[k, i : i + 1] = coef1[k][i]
    one, zero = jnp.ones((1, 256), F32), jnp.zeros((1, 256), F32)
    basis = []
    for ends in ((one, zero), (zero, one)):
        basis.append(fill_chain(coef, None, *stack_ends(fill_chain(coef1, None, *ends))))
    for k in range(2):
        for i in range(STEPS):
            fields_ref[6 + k, i] = basis[k][i]
    gather_ref[0:1] = first1
    gather_ref[1:2] = last1
    gather_ref[2:3] = link1
    gather_ref[3:4] = both(lambda h: turned[1, h, 127:128, :] * turned[4, h, 127:128, :])
    gather_ref[4:5] = both(lambda h: turned[4, h, 0:1, :])
    for row, weight, move in ((5, crosses, cross_next), (9, verts, layer_next)):
        sums = [jnp.zeros((SUBS, 256), F32)] * 4
        for i in range(STEPS):
            moved = [move(basis[k][i]) for k in range(2)]
            for a in range(2):
                weighted = weight[i] * basis[a][i]
                for b in range(2):
                    sums[2 * a + b] = sums[2 * a + b] + weighted * moved[b]
        for k in range(4):
            gather_ref[row + k : row + k + 1] = column_sum(sums[k])


def load_coef(fields_ref, small_ref):
    coef = tuple([None] + [fields_ref[3 + k, i] for i in range(1, STEPS - 1)] + [None] for k in range(3))
    coef1 = tuple([None] + [small_ref[k, i : i + 1] for i in range(1, 2 * SUBS - 1)] + [None] for k in range(3))
    return coef, coef1


def local_solve(coef, coef1, rhs, first, last):
    part, ends_first, ends_last = reduce_source(coef[1], coef[2], rhs)
    part1, source_first, source_last = reduce_source(coef1[1], coef1[2], interleave(ends_first, ends_last))
    ends = stack_ends(fill_chain(coef1, part1, first, last))
    return fill_chain(coef, part, *ends), source_first, source_last


def source_kernel(fields_ref, small_ref, base_ref, own_ref, low_ref, high_ref, coefs_ref,
                  source_ref, inner_ref, out_ref, rain_scratch):
    rain_scratch[...] = own_ref[...] + low_ref[...] + high_ref[...]
    coef, coef1 = load_coef(fields_ref, small_ref)
    top = lax.broadcasted_iota(jnp.int32, (SUBS, 128), 1) < 64
    zero = jnp.zeros((1, 256), F32)
    none = jnp.zeros((SUBS, 128), F32)
    rows = []
    for s in range(2):
        rhs = []
        for i in range(STEPS):
            water = rain_scratch[step_rows(i), :]
            if s:
                water = pltpu.roll(water, 64, 1)
            water = jnp.concatenate([jnp.where(top, water, 0.0), none], axis=1) * fields_ref[2, i]
            source_ref[s, i] = base_ref[s, i] + water
            rhs.append(base_ref[2 + s, i] + water)
        inner, first, last = local_solve(coef, coef1, rhs, zero, zero)
        sums = [jnp.zeros((SUBS, 256), F32)] * 2
        for i in range(STEPS):
            inner_ref[s, i] = inner[i]
            later = source_ref[s, i] + coupled(fields_ref[0, i], fields_ref[1, i], inner[i])
            for k in range(2):
                sums[k] = sums[k] + fields_ref[6 + k, i] * later
        rows += [first, last, column_sum(sums[0]), column_sum(sums[1])]
    put_block(out_ref, [coefs_ref[k : k + 1] for k in range(13)] + rows)


def put_block(ref, rows):
    for k in range(ROWS):
        row = rows[k] if k < len(rows) else jnp.zeros((1, 256), F32)
        for h in range(2):
            ref[ROWS * h + k : ROWS * h + k + 1] = row[:, 128 * h : 128 * h + 128]


def coupled_ends(got, later, low, high):
    for row, ahead, back in ((5, cross_next, cross_prev), (9, layer_next, layer_prev)):
        k = [got(row + m) for m in range(4)]
        low_ahead, high_ahead = ahead(low), ahead(high)
        later = (
            later[0] + k[0] * low_ahead + k[1] * high_ahead + back(k[0] * low + k[2] * high),
            later[1] + k[2] * low_ahead + k[3] * high_ahead + back(k[1] * low + k[3] * high),
        )
    return later


def member(blocks_ref, p):
    return lambda row: both(lambda h: blocks_ref[p, ROWS * h + row : ROWS * h + row + 1, :])


def group_later(blocks_ref, s, nodes):
    out = []
    for p in range(blocks_ref.shape[0]):
        got = member(blocks_ref, p)
        out += coupled_ends(got, (got(15 + 4 * s), got(16 + 4 * s)), nodes[2 * p], nodes[2 * p + 1])
    return out


def group_kernel(place_ref, own_ref, from1_ref, from2_ref, from3_ref, blocks_ref, saved_ref, out_ref, block):
    per = blocks_ref.shape[0]
    place = lax.rem(place_ref[0], per)
    for k, ref in enumerate((own_ref, from1_ref, from2_ref, from3_ref)):
        blocks_ref[lax.rem(place + per - k, per)] = ref[...]
    got = [member(blocks_ref, p) for p in range(per)]
    leak, face = [], []
    for p in range(per):
        leak += [got[p](0), got[p](1)]
        face.append(got[p](2))
        if p + 1 < per:
            face.append(got[p](3) * got[p + 1](4))
    coef, first, last, link = reduce_chain(leak, face)
    nodes = 2 * per
    one, zero = jnp.ones((1, 256), F32), jnp.zeros((1, 256), F32)
    basis = [fill_chain(coef, None, one, zero), fill_chain(coef, None, zero, one)]
    for k in range(3):
        for i in range(1, nodes - 1):
            saved_ref[nodes * k + i : nodes * k + i + 1] = coef[k][i]
    rows = [first, last, link, got[per - 1](3), got[0](4)]
    for row, move in ((5, cross_next), (9, layer_next)):
        sums = [zero] * 4
        for p in range(per):
            moved = [[move(basis[b][2 * p + e]) for e in range(2)] for b in range(2)]
            k = [got[p](row + m) for m in range(4)]
            for b in range(2):
                ends = [k[2 * e] * moved[b][0] + k[2 * e + 1] * moved[b][1] for e in range(2)]
                for a in range(2):
                    sums[2 * a + b] = sums[2 * a + b] + basis[a][2 * p] * ends[0] + basis[a][2 * p + 1] * ends[1]
        rows += sums
    for s in range(2):
        rhs = [got[p](13 + 4 * s + e) for p in range(per) for e in range(2)]
        part, source_first, source_last = reduce_source(coef[1], coef[2], rhs)
        inner = fill_chain(coef, part, zero, zero)
        _, later_first, later_last = reduce_source(coef[1], coef[2], group_later(blocks_ref, s, inner))
        rows += [source_first, source_last, later_first, later_last]
        for i in range(nodes):
            saved_ref[nodes * (5 + s) + i : nodes * (5 + s) + i + 1] = inner[i]
            saved_ref[nodes * (3 + s) + i : nodes * (3 + s) + i + 1] = basis[s][i]
    put_block(block, rows)
    for k in range(out_ref.shape[0]):
        out_ref[k] = block[...]


def sweep_kernel(place_ref, gathered_ref, blocks_ref, saved_ref, fields_ref, small_ref, source_ref, inner_ref,
                 head_ref, total_ref, ends_scratch, turned):
    per = blocks_ref.shape[0]
    groups = gathered_ref.shape[0] // (2 * ROWS)
    place = place_ref[0]

    def got(row):
        return both(lambda h: gathered_ref[pl.ds(ROWS * h + row, groups, stride=2 * ROWS), :])

    face = got(3) * pltpu.roll(got(4), groups - 1, 0)
    inv, ratio = full_factor(interleave(got(0), got(1)), interleave(got(2), face)[: 2 * groups - 1])
    nodes = 2 * per
    saved = [[saved_ref[nodes * k + i : nodes * k + i + 1] for i in range(nodes)] for k in range(7)]
    at = pl.ds(place // per, 1)
    pick = pl.ds(lax.rem(place, per), 1)
    ends = []
    for s in range(2):
        row = 13 + 4 * s
        low, high = stack_ends(full_solve(inv, ratio, interleave(got(row), got(row + 1))))
        later = coupled_ends(got, (got(row + 2), got(row + 3)), low, high)
        low2, high2 = stack_ends(full_solve(inv, ratio, interleave(*later)))
        for k, value in enumerate((low, high, low2, high2)):
            ends_scratch[k] = value
        low, high, low2, high2 = [ends_scratch[k, at, :] for k in range(4)]
        first = [saved[5 + s][i] + saved[3][i] * low + saved[4][i] * high for i in range(nodes)]
        part, _, _ = reduce_source(saved[1], saved[2], group_later(blocks_ref, s, first))
        second = fill_chain(tuple(saved[:3]), part, low2, high2)
        for k, values in enumerate((first[0::2], first[1::2], second[0::2], second[1::2])):
            for p in range(per):
                ends_scratch[k, p : p + 1] = values[p]
        ends.append([ends_scratch[k, pick, :] for k in range(4)])
    coef, coef1 = load_coef(fields_ref, small_ref)
    for s in range(2):
        low1, high1, low2, high2 = ends[s]
        rhs = []
        for i in range(STEPS):
            head = inner_ref[s, i] + fields_ref[6, i] * low1 + fields_ref[7, i] * high1
            rhs.append(source_ref[s, i] + coupled(fields_ref[0, i], fields_ref[1, i], head))
        solved, _, _ = local_solve(coef, coef1, rhs, low2, high2)
        for i in range(STEPS):
            for h in range(2):
                turned[s, h, step_rows(i), :] = solved[i][:, 128 * h : 128 * h + 128]
    for h in range(2):
        lanes = [turned[s, h].T for s in range(2)]
        for s in range(2):
            head_ref[s, 2 * h : 2 * h + 2] = lanes[s].reshape(2, 64, 128)
        total_ref[2 * h : 2 * h + 2] = (lanes[0] + lanes[1]).reshape(2, 64, 128)


VMEM = pl.BlockSpec(memory_space=pltpu.VMEM)
SMEM = pl.BlockSpec(memory_space=pltpu.SMEM)


def kernel_call(body, name, specs, outs, scratch, flops):
    return pl.pallas_call(
        body,
        name=name,
        in_specs=specs,
        out_specs=[VMEM] * len(outs),
        out_shape=[jax.ShapeDtypeStruct(shape, F32) for shape in outs],
        scratch_shapes=[pltpu.VMEM(shape, F32) for shape in scratch],
        compiler_params=pltpu.CompilerParams(vmem_limit_bytes=48 * 2**20),
        cost_estimate=pl.CostEstimate(flops=flops, bytes_accessed=2 * 2**20, transcendentals=0),
    )


def on_device(
    head_prev,
    storage,
    cond_flow,
    cond_cross,
    cond_vert,
    active,
    hru_cells,
    hru_area,
    hru_land,
    hru_bmp,
    rain,
    perc_table,
    hru_live,
):
    slots = hru_land.shape[0]
    devices = lax.axis_size("flow")
    tile = (128, 128)
    blocks = [(4, slots), (4, slots), (1, slots), (2, slots), (1, slots), (8, 16)]
    before, own, after = pl.pallas_call(
        scatter_kernel,
        name="scatter",
        grid=(1,),
        in_specs=[pl.BlockSpec(shape, lambda i: (0, 0)) for shape in blocks] + [SMEM],
        out_specs=[pl.BlockSpec(tile, lambda i: (0, 0))] * 3,
        out_shape=[jax.ShapeDtypeStruct(tile, F32)] * 3,
        scratch_shapes=[pltpu.VMEM((4, 4, slots), F32), pltpu.VMEM((3,) + tile, F32)],
        compiler_params=pltpu.CompilerParams(vmem_limit_bytes=60 * 2**20),
        cost_estimate=pl.CostEstimate(flops=4 * 10**9, bytes_accessed=2 * 2**20, transcendentals=0),
    )(
        hru_cells.T, hru_area.T, hru_land.reshape(1, slots), hru_bmp, rain.reshape(1, slots), perc_table.T, hru_live
    )
    high = lax.ppermute(before, "flow", [(i + 1, i) for i in range(devices - 1)])
    low = lax.ppermute(after, "flow", [(i, i + 1) for i in range(devices - 1)])
    fields, small, base, coefs = kernel_call(
        coefficient_kernel,
        "coefficients",
        [VMEM] * 6,
        [(8, STEPS, SUBS, 256), (3, 2 * SUBS, 256), (4, STEPS, SUBS, 256), (16, 256)],
        [(7, 2, 128, 128)],
        4 * 10**9,
    )(head_prev, storage, cond_flow, cond_cross, cond_vert, active)
    source, inner, block = kernel_call(
        source_kernel,
        "sources",
        [VMEM] * 7,
        [(2, STEPS, SUBS, 256), (2, STEPS, SUBS, 256), (2 * ROWS, 128)],
        [tile],
        10**9,
    )(fields, small, base, own, low, high, coefs)
    place = lax.axis_index("flow").astype(jnp.int32).reshape(1)
    per = devices // SUBS
    around = [
        lax.ppermute(block, "flow", [(i, i - i % per + (i + k) % per) for i in range(devices)]) for k in range(1, per)
    ]
    blocks, saved, block = kernel_call(
        group_kernel,
        "groups",
        [SMEM] + [VMEM] * per,
        [(per, 2 * ROWS, 128), (14 * per, 256), (SUBS, 2 * ROWS, 128)],
        [(2 * ROWS, 128)],
        10**9,
    )(place, block, *around)
    same = [[i + per * k for k in range(SUBS)] for i in range(per)]
    gathered = lax.all_to_all(block, "flow", split_axis=0, concat_axis=0, axis_index_groups=same, tiled=True)
    head, total = kernel_call(
        sweep_kernel,
        "sweeps",
        [SMEM] + [VMEM] * 7,
        [head_prev.shape, storage.shape],
        [(4, SUBS, 256), (2, 2, 128, 128)],
        10**9,
    )(place, gathered.reshape(SUBS * 2 * ROWS, 128), blocks, saved, fields, small, source, inner)
    lanes = lax.axis_size("lane")
    whole = total
    for k in range(2, lanes, 2):
        whole = whole + lax.ppermute(total, "lane", [(i, (i + k) % lanes) for i in range(lanes)])
    whole = whole + lax.ppermute(whole, "lane", [(i, i ^ 1) for i in range(lanes)])
    anomaly = head - whole[None] / (2 * lanes)
    return head, anomaly


def solution(mesh):
    return jax.shard_map(
        on_device,
        mesh=mesh,
        in_specs=(
            P("lane", None, None, "flow"),
            P(None, None, "flow"),
            P(None, None, "flow"),
            P(None, None, "flow"),
            P(None, None, "flow"),
            P(None, None, "flow"),
            P("flow", None),
            P("flow", None),
            P("flow"),
            P("lane", "flow"),
            P("flow"),
            P(),
            P("flow"),
        ),
        out_specs=(P("lane", None, None, "flow"), P("lane", None, None, "flow")),
        check_vma=False,
    )
```

```python
import functools

import jax
import jax.numpy as jnp
from jax import lax
from jax.experimental import pallas as pl
from jax.experimental.pallas import tpu as pltpu
from jax.sharding import PartitionSpec as P

STEPS = 16
SUBS = 8
ROWS = 24
F32 = jnp.float32
BF16 = jnp.bfloat16


def halves(fn, a):
    return jnp.concatenate([fn(a[:, :128]), fn(a[:, 128:])], axis=1)


def cross_next(a):
    return halves(lambda h: pltpu.roll(h, 127, 1), a)


def cross_prev(a):
    return halves(lambda h: pltpu.roll(h, 1, 1), a)


def layer_rolls(a):
    lo = lax.broadcasted_iota(jnp.int32, (a.shape[0], 128), 1) < 64
    return lo, pltpu.roll(a[:, :128], 64, 1), pltpu.roll(a[:, 128:], 64, 1)


def layer_next(a):
    lo, r0, r1 = layer_rolls(a)
    return jnp.concatenate([jnp.where(lo, r0, r1), jnp.where(lo, r1, r0)], axis=1)


def layer_prev(a):
    lo, r0, r1 = layer_rolls(a)
    return jnp.concatenate([jnp.where(lo, r1, r0), jnp.where(lo, r0, r1)], axis=1)


def coupled(cross, vert, head):
    out = cross * cross_next(head) + cross_prev(cross * head)
    return out + vert * layer_next(head) + layer_prev(vert * head)


def reduce_chain(leak, face):
    n = len(leak)
    first, link, shunt = leak[0], face[0], leak[1]
    inv, ratio, share = [None] * n, [None] * n, [None] * n
    for i in range(1, n - 1):
        inv[i] = 1.0 / (face[i] + (shunt + link))
        ratio[i] = face[i] * inv[i]
        share[i] = link * inv[i]
        first = first + shunt * share[i]
        shunt = leak[i + 1] + shunt * ratio[i]
        link = link * ratio[i]
    return (inv, ratio, share), first, shunt, link


def reduce_source(ratio, share, rhs):
    n = len(rhs)
    first = rhs[0]
    part = [None] * n
    part[1] = rhs[1]
    for i in range(1, n - 1):
        first = first + share[i] * part[i]
        part[i + 1] = rhs[i + 1] + ratio[i] * part[i]
    return part, first, part[n - 1]


def fill_chain(coef, part, first, last):
    inv, ratio, share = coef
    n = len(ratio)
    out = [None] * n
    out[0], out[n - 1] = first, last
    for i in range(n - 2, 0, -1):
        value = share[i] * first + ratio[i] * out[i + 1]
        out[i] = value if part is None else value + inv[i] * part[i]
    return out


def full_factor(leak, face):
    n = len(leak)
    shunt = leak[0]
    inv, ratio = [None] * n, [None] * n
    for i in range(n - 1):
        inv[i] = 1.0 / (face[i] + shunt)
        ratio[i] = face[i] * inv[i]
        shunt = leak[i + 1] + shunt * ratio[i]
    inv[n - 1] = 1.0 / shunt
    return inv, ratio


def full_solve(inv, ratio, rhs):
    n = len(rhs)
    part = [rhs[0]]
    for i in range(n - 1):
        part.append(rhs[i + 1] + ratio[i] * part[i])
    out = [None] * n
    out[n - 1] = inv[n - 1] * part[n - 1]
    for i in range(n - 2, -1, -1):
        out[i] = inv[i] * part[i] + ratio[i] * out[i + 1]
    return out


def to_rows(a):
    return [a[k : k + 1] for k in range(SUBS)]


def interleave(a, b):
    return [x for pair in zip(to_rows(a), to_rows(b)) for x in pair]


def stack_ends(nodes):
    return jnp.concatenate(nodes[0::2], axis=0), jnp.concatenate(nodes[1::2], axis=0)


def column_sum(a):
    return jnp.sum(a, axis=0, keepdims=True)


def both(fn):
    return jnp.concatenate([fn(0), fn(1)], axis=1)


def step_rows(i):
    return pl.ds(i, SUBS, stride=STEPS)


def scatter_kernel(cells_ref, area_ref, land_ref, bmp_ref, rain_ref, table_ref, live_ref,
                   place_ref, first_ref, own_ref, second_ref, amount_ref, window_ref):
    slots = land_ref.shape[1]
    land = land_ref[...]
    rates = jnp.zeros((8, slots), F32)
    for use in range(table_ref.shape[1]):
        rates = jnp.where(land == use, table_ref[:, use : use + 1], rates)
    bmp = bmp_ref[...]
    chosen = jnp.zeros(bmp.shape, F32)
    for code in range(table_ref.shape[0]):
        chosen = jnp.where(bmp == code, rates[code : code + 1], chosen)
    alive = lax.broadcasted_iota(jnp.int32, (1, slots), 1) < live_ref[0]
    perc = jnp.where(alive, rain_ref[...] * chosen, 0.0)
    for q in range(4):
        amount = perc * area_ref[q : q + 1, :]
        high = amount.astype(BF16).astype(F32)
        amount_ref[q, 0:2, :] = high
        amount_ref[q, 2:4, :] = amount - high
    column = lax.broadcasted_iota(jnp.int32, (256, slots), 0).astype(F32).astype(BF16)
    line = lax.broadcasted_iota(jnp.int32, (96, slots), 0).astype(F32).astype(BF16)
    one, zero = jnp.ones((), BF16), jnp.zeros((), BF16)
    total = None
    for q in range(4):
        cell = cells_ref[q : q + 1, :]
        columns = jnp.where(column == (cell & 255).astype(F32).astype(BF16), one, zero)
        hit = line == (cell >> 8).astype(F32).astype(BF16)
        put = [jnp.where(hit, amount_ref[q, k : k + 1, :].astype(BF16), zero) for k in (0, 2, 1, 3)]
        product = lax.dot_general(
            jnp.concatenate(put, axis=0), columns, (((1,), (1,)), ((), ())), preferred_element_type=F32
        )
        total = product if total is None else total + product
    for s in range(2):
        summed = total[192 * s : 192 * s + 96] + total[192 * s + 96 : 192 * s + 192]
        for k in range(3):
            for odd in range(2):
                window_ref[k, pl.ds(64 * s + odd, 32, stride=2), :] = summed[
                    32 * k : 32 * k + 32, 128 * odd : 128 * odd + 128
                ]
    odd = lax.rem(place_ref[0], 2)
    own_ref[...] = window_ref[1].T
    first_ref[...] = window_ref[2 - 2 * odd].T
    second_ref[...] = window_ref[2 * odd].T


def coefficient_kernel(head_ref, storage_ref, flow_ref, cross_ref, vert_ref, active_ref,
                       fields_ref, small_ref, base_ref, gather_ref, turned):
    def turn(slot, part):
        for h in range(2):
            turned[slot, h] = part(h).T

    for slot, ref in enumerate((storage_ref, flow_ref, cross_ref, vert_ref)):
        turn(slot, lambda h: ref[2 * h : 2 * h + 2].reshape(128, 128))
    turn(4, lambda h: active_ref[2 * h : 2 * h + 2].reshape(128, 128).astype(F32))
    for s in range(2):
        turn(5 + s, lambda h: head_ref[s, 2 * h : 2 * h + 2].reshape(128, 128))

    def step(slot, i):
        return both(lambda h: turned[slot, h, step_rows(i), :])

    lane = lax.broadcasted_iota(jnp.int32, (SUBS, 256), 1)
    inner_cross = lane % 64 != 63
    inner_vert = lane < 192
    mask = [step(4, i) for i in range(STEPS)]
    leak, face, crosses, verts = [], [], [], []
    for i in range(STEPS):
        m = mask[i]
        cross = jnp.where(inner_cross, step(2, i) * m * cross_next(m), 0.0)
        vert = jnp.where(inner_vert, step(3, i) * m * layer_next(m), 0.0)
        store = step(0, i)
        leak.append(store + cross + cross_prev(cross) + vert + layer_prev(vert))
        after = mask[i + 1] if i + 1 < STEPS else pltpu.roll(mask[0], SUBS - 1, 0)
        face.append(step(1, i) * m * after)
        crosses.append(cross)
        verts.append(vert)
        fields_ref[0, i] = cross
        fields_ref[1, i] = vert
        fields_ref[2, i] = m
        for s in range(2):
            head = step(5 + s, i)
            base = store * head
            base_ref[s, i] = base
            base_ref[2 + s, i] = base + coupled(cross, vert, head)
    coef, first, last, link = reduce_chain(leak, face[: STEPS - 1])
    leak1 = interleave(first, last)
    face1 = interleave(link, face[STEPS - 1])[: 2 * SUBS - 1]
    coef1, first1, last1, link1 = reduce_chain(leak1, face1)
    for k in range(3):
        for i in range(1, STEPS - 1):
            fields_ref[3 + k, i] = coef[k][i]
        for i in range(1, 2 * SUBS - 1):
            small_ref[k, i : i + 1] = coef1[k][i]
    one, zero = jnp.ones((1, 256), F32), jnp.zeros((1, 256), F32)
    basis = []
    for ends in ((one, zero), (zero, one)):
        basis.append(fill_chain(coef, None, *stack_ends(fill_chain(coef1, None, *ends))))
    for k in range(2):
        for i in range(STEPS):
            fields_ref[6 + k, i] = basis[k][i]
    gather_ref[0:1] = first1
    gather_ref[1:2] = last1
    gather_ref[2:3] = link1
    gather_ref[3:4] = both(lambda h: turned[1, h, 127:128, :] * turned[4, h, 127:128, :])
    gather_ref[4:5] = both(lambda h: turned[4, h, 0:1, :])
    for row, weight, move in ((5, crosses, cross_next), (9, verts, layer_next)):
        sums = [jnp.zeros((SUBS, 256), F32)] * 4
        for i in range(STEPS):
            moved = [move(basis[k][i]) for k in range(2)]
            for a in range(2):
                weighted = weight[i] * basis[a][i]
                for b in range(2):
                    sums[2 * a + b] = sums[2 * a + b] + weighted * moved[b]
        for k in range(4):
            gather_ref[row + k : row + k + 1] = column_sum(sums[k])


def load_coef(fields_ref, small_ref):
    coef = tuple([None] + [fields_ref[3 + k, i] for i in range(1, STEPS - 1)] + [None] for k in range(3))
    coef1 = tuple([None] + [small_ref[k, i : i + 1] for i in range(1, 2 * SUBS - 1)] + [None] for k in range(3))
    return coef, coef1


def local_solve(coef, coef1, rhs, first, last):
    part, ends_first, ends_last = reduce_source(coef[1], coef[2], rhs)
    part1, source_first, source_last = reduce_source(coef1[1], coef1[2], interleave(ends_first, ends_last))
    ends = stack_ends(fill_chain(coef1, part1, first, last))
    return fill_chain(coef, part, *ends), source_first, source_last


def source_kernel(fields_ref, small_ref, base_ref, own_ref, low_ref, high_ref, coefs_ref,
                  source_ref, inner_ref, out_ref, rain_scratch):
    rain_scratch[...] = own_ref[...] + low_ref[...] + high_ref[...]
    coef, coef1 = load_coef(fields_ref, small_ref)
    top = lax.broadcasted_iota(jnp.int32, (SUBS, 128), 1) < 64
    zero = jnp.zeros((1, 256), F32)
    none = jnp.zeros((SUBS, 128), F32)
    rows = []
    for s in range(2):
        rhs = []
        for i in range(STEPS):
            water = rain_scratch[step_rows(i), :]
            if s:
                water = pltpu.roll(water, 64, 1)
            water = jnp.concatenate([jnp.where(top, water, 0.0), none], axis=1) * fields_ref[2, i]
            source_ref[s, i] = base_ref[s, i] + water
            rhs.append(base_ref[2 + s, i] + water)
        inner, first, last = local_solve(coef, coef1, rhs, zero, zero)
        sums = [jnp.zeros((SUBS, 256), F32)] * 2
        for i in range(STEPS):
            inner_ref[s, i] = inner[i]
            later = source_ref[s, i] + coupled(fields_ref[0, i], fields_ref[1, i], inner[i])
            for k in range(2):
                sums[k] = sums[k] + fields_ref[6 + k, i] * later
        rows += [first, last, column_sum(sums[0]), column_sum(sums[1])]
    put_block(out_ref, [coefs_ref[k : k + 1] for k in range(13)] + rows)


def put_block(ref, rows):
    for k in range(ROWS):
        row = rows[k] if k < len(rows) else jnp.zeros((1, 256), F32)
        for h in range(2):
            ref[ROWS * h + k : ROWS * h + k + 1] = row[:, 128 * h : 128 * h + 128]


def coupled_ends(got, later, low, high):
    for row, ahead, back in ((5, cross_next, cross_prev), (9, layer_next, layer_prev)):
        k = [got(row + m) for m in range(4)]
        low_ahead, high_ahead = ahead(low), ahead(high)
        later = (
            later[0] + k[0] * low_ahead + k[1] * high_ahead + back(k[0] * low + k[2] * high),
            later[1] + k[2] * low_ahead + k[3] * high_ahead + back(k[1] * low + k[3] * high),
        )
    return later


def member(blocks_ref, p):
    return lambda row: both(lambda h: blocks_ref[p, ROWS * h + row : ROWS * h + row + 1, :])


def group_later(blocks_ref, s, nodes):
    out = []
    for p in range(blocks_ref.shape[0]):
        got = member(blocks_ref, p)
        out += coupled_ends(got, (got(15 + 4 * s), got(16 + 4 * s)), nodes[2 * p], nodes[2 * p + 1])
    return out


def group_kernel(place_ref, own_ref, from1_ref, from2_ref, from3_ref, blocks_ref, saved_ref, out_ref, block):
    per = blocks_ref.shape[0]
    place = lax.rem(place_ref[0], per)
    for k, ref in enumerate((own_ref, from1_ref, from2_ref, from3_ref)):
        blocks_ref[lax.bitwise_xor(place, k)] = ref[...]
    got = [member(blocks_ref, p) for p in range(per)]
    leak, face = [], []
    for p in range(per):
        leak += [got[p](0), got[p](1)]
        face.append(got[p](2))
        if p + 1 < per:
            face.append(got[p](3) * got[p + 1](4))
    coef, first, last, link = reduce_chain(leak, face)
    nodes = 2 * per
    one, zero = jnp.ones((1, 256), F32), jnp.zeros((1, 256), F32)
    basis = [fill_chain(coef, None, one, zero), fill_chain(coef, None, zero, one)]
    for k in range(3):
        for i in range(1, nodes - 1):
            saved_ref[nodes * k + i : nodes * k + i + 1] = coef[k][i]
    rows = [first, last, link, got[per - 1](3), got[0](4)]
    for row, move in ((5, cross_next), (9, layer_next)):
        sums = [zero] * 4
        for p in range(per):
            moved = [[move(basis[b][2 * p + e]) for e in range(2)] for b in range(2)]
            k = [got[p](row + m) for m in range(4)]
            for b in range(2):
                ends = [k[2 * e] * moved[b][0] + k[2 * e + 1] * moved[b][1] for e in range(2)]
                for a in range(2):
                    sums[2 * a + b] = sums[2 * a + b] + basis[a][2 * p] * ends[0] + basis[a][2 * p + 1] * ends[1]
        rows += sums
    for s in range(2):
        rhs = [got[p](13 + 4 * s + e) for p in range(per) for e in range(2)]
        part, source_first, source_last = reduce_source(coef[1], coef[2], rhs)
        inner = fill_chain(coef, part, zero, zero)
        _, later_first, later_last = reduce_source(coef[1], coef[2], group_later(blocks_ref, s, inner))
        rows += [source_first, source_last, later_first, later_last]
        for i in range(nodes):
            saved_ref[nodes * (5 + s) + i : nodes * (5 + s) + i + 1] = inner[i]
            saved_ref[nodes * (3 + s) + i : nodes * (3 + s) + i + 1] = basis[s][i]
    put_block(block, rows)
    for k in range(out_ref.shape[0]):
        out_ref[k] = block[...]


def sweep_kernel(place_ref, gathered_ref, blocks_ref, saved_ref, fields_ref, small_ref, source_ref, inner_ref,
                 head_ref, total_ref, ends_scratch, turned):
    per = blocks_ref.shape[0]
    groups = gathered_ref.shape[0] // (2 * ROWS)
    place = place_ref[0]

    def got(row):
        return both(lambda h: gathered_ref[pl.ds(ROWS * h + row, groups, stride=2 * ROWS), :])

    face = got(3) * pltpu.roll(got(4), groups - 1, 0)
    inv, ratio = full_factor(interleave(got(0), got(1)), interleave(got(2), face)[: 2 * groups - 1])
    nodes = 2 * per
    saved = [[saved_ref[nodes * k + i : nodes * k + i + 1] for i in range(nodes)] for k in range(7)]
    at = pl.ds(place // per, 1)
    pick = pl.ds(lax.rem(place, per), 1)
    ends = []
    for s in range(2):
        row = 13 + 4 * s
        low, high = stack_ends(full_solve(inv, ratio, interleave(got(row), got(row + 1))))
        later = coupled_ends(got, (got(row + 2), got(row + 3)), low, high)
        low2, high2 = stack_ends(full_solve(inv, ratio, interleave(*later)))
        for k, value in enumerate((low, high, low2, high2)):
            ends_scratch[k] = value
        low, high, low2, high2 = [ends_scratch[k, at, :] for k in range(4)]
        first = [saved[5 + s][i] + saved[3][i] * low + saved[4][i] * high for i in range(nodes)]
        part, _, _ = reduce_source(saved[1], saved[2], group_later(blocks_ref, s, first))
        second = fill_chain(tuple(saved[:3]), part, low2, high2)
        for k, values in enumerate((first[0::2], first[1::2], second[0::2], second[1::2])):
            for p in range(per):
                ends_scratch[k, p : p + 1] = values[p]
        ends.append([ends_scratch[k, pick, :] for k in range(4)])
    coef, coef1 = load_coef(fields_ref, small_ref)
    for s in range(2):
        low1, high1, low2, high2 = ends[s]
        rhs = []
        for i in range(STEPS):
            head = inner_ref[s, i] + fields_ref[6, i] * low1 + fields_ref[7, i] * high1
            rhs.append(source_ref[s, i] + coupled(fields_ref[0, i], fields_ref[1, i], head))
        solved, _, _ = local_solve(coef, coef1, rhs, low2, high2)
        for i in range(STEPS):
            for h in range(2):
                turned[s, h, step_rows(i), :] = solved[i][:, 128 * h : 128 * h + 128]
    for h in range(2):
        lanes = [turned[s, h].T for s in range(2)]
        for s in range(2):
            head_ref[s, 2 * h : 2 * h + 2] = lanes[s].reshape(2, 64, 128)
        total_ref[2 * h : 2 * h + 2] = (lanes[0] + lanes[1]).reshape(2, 64, 128)


VMEM = pl.BlockSpec(memory_space=pltpu.VMEM)
SMEM = pl.BlockSpec(memory_space=pltpu.SMEM)


def kernel_call(body, name, specs, outs, scratch, flops):
    return pl.pallas_call(
        body,
        name=name,
        in_specs=specs,
        out_specs=[VMEM] * len(outs),
        out_shape=[jax.ShapeDtypeStruct(shape, F32) for shape in outs],
        scratch_shapes=[pltpu.VMEM(shape, F32) for shape in scratch],
        compiler_params=pltpu.CompilerParams(vmem_limit_bytes=48 * 2**20),
        cost_estimate=pl.CostEstimate(flops=flops, bytes_accessed=2 * 2**20, transcendentals=0),
    )


def on_device(
    head_prev,
    storage,
    cond_flow,
    cond_cross,
    cond_vert,
    active,
    hru_cells,
    hru_area,
    hru_land,
    hru_bmp,
    rain,
    perc_table,
    hru_live,
):
    slots = hru_land.shape[0]
    devices = lax.axis_size("flow")
    tile = (128, 128)
    blocks = [(4, slots), (4, slots), (1, slots), (2, slots), (1, slots), (8, 16)]
    place = lax.axis_index("flow").astype(jnp.int32).reshape(1)
    first, own, second = pl.pallas_call(
        scatter_kernel,
        name="scatter",
        grid=(1,),
        in_specs=[pl.BlockSpec(shape, lambda i: (0, 0)) for shape in blocks] + [SMEM] * 2,
        out_specs=[pl.BlockSpec(tile, lambda i: (0, 0))] * 3,
        out_shape=[jax.ShapeDtypeStruct(tile, F32)] * 3,
        scratch_shapes=[pltpu.VMEM((4, 4, slots), F32), pltpu.VMEM((3,) + tile, F32)],
        compiler_params=pltpu.CompilerParams(vmem_limit_bytes=60 * 2**20),
        cost_estimate=pl.CostEstimate(flops=4 * 10**9, bytes_accessed=2 * 2**20, transcendentals=0),
    )(
        hru_cells.T, hru_area.T, hru_land.reshape(1, slots), hru_bmp, rain.reshape(1, slots), perc_table.T, hru_live, place
    )
    low = lax.ppermute(first, "flow", [(i, i ^ 1) for i in range(devices)])
    high = lax.ppermute(second, "flow", [(i, i - 1 + 2 * (i % 2)) for i in range(1, devices - 1)])
    fields, small, base, coefs = kernel_call(
        coefficient_kernel,
        "coefficients",
        [VMEM] * 6,
        [(8, STEPS, SUBS, 256), (3, 2 * SUBS, 256), (4, STEPS, SUBS, 256), (16, 256)],
        [(7, 2, 128, 128)],
        4 * 10**9,
    )(head_prev, storage, cond_flow, cond_cross, cond_vert, active)
    source, inner, block = kernel_call(
        source_kernel,
        "sources",
        [VMEM] * 7,
        [(2, STEPS, SUBS, 256), (2, STEPS, SUBS, 256), (2 * ROWS, 128)],
        [tile],
        10**9,
    )(fields, small, base, own, low, high, coefs)
    per = devices // SUBS
    around = [
        lax.ppermute(block, "flow", [(i, i ^ k) for i in range(devices)]) for k in range(1, per)
    ]
    blocks, saved, block = kernel_call(
        group_kernel,
        "groups",
        [SMEM] + [VMEM] * per,
        [(per, 2 * ROWS, 128), (14 * per, 256), (SUBS, 2 * ROWS, 128)],
        [(2 * ROWS, 128)],
        10**9,
    )(place, block, *around)
    same = [[i + per * k for k in range(SUBS)] for i in range(per)]
    gathered = lax.all_to_all(block, "flow", split_axis=0, concat_axis=0, axis_index_groups=same, tiled=True)
    head, total = kernel_call(
        sweep_kernel,
        "sweeps",
        [SMEM] + [VMEM] * 7,
        [head_prev.shape, storage.shape],
        [(4, SUBS, 256), (2, 2, 128, 128)],
        10**9,
    )(place, gathered.reshape(SUBS * 2 * ROWS, 128), blocks, saved, fields, small, source, inner)
    lanes = lax.axis_size("lane")
    whole = total
    for k in range(2, lanes, 2):
        whole = whole + lax.ppermute(total, "lane", [(i, i ^ k) for i in range(lanes)])
    whole = whole + lax.ppermute(whole, "lane", [(i, i ^ 1) for i in range(lanes)])
    anomaly = head - whole[None] / (2 * lanes)
    return head, anomaly


def solution(mesh):
    return jax.shard_map(
        on_device,
        mesh=mesh,
        in_specs=(
            P("lane", None, None, "flow"),
            P(None, None, "flow"),
            P(None, None, "flow"),
            P(None, None, "flow"),
            P(None, None, "flow"),
            P(None, None, "flow"),
            P("flow", None),
            P("flow", None),
            P("flow"),
            P("lane", "flow"),
            P("flow"),
            P(),
            P("flow"),
        ),
        out_specs=(P("lane", None, None, "flow"), P("lane", None, None, "flow")),
        check_vma=False,
    )
```

```python
import functools

import jax
import jax.numpy as jnp
from jax import lax
from jax.experimental import pallas as pl
from jax.experimental.pallas import tpu as pltpu
from jax.sharding import PartitionSpec as P

STEPS = 16
SUBS = 8
ROWS = 24
F32 = jnp.float32
BF16 = jnp.bfloat16


def halves(fn, a):
    return jnp.concatenate([fn(a[:, :128]), fn(a[:, 128:])], axis=1)


def cross_next(a):
    return halves(lambda h: pltpu.roll(h, 127, 1), a)


def cross_prev(a):
    return halves(lambda h: pltpu.roll(h, 1, 1), a)


def layer_rolls(a):
    lo = lax.broadcasted_iota(jnp.int32, (a.shape[0], 128), 1) < 64
    return lo, pltpu.roll(a[:, :128], 64, 1), pltpu.roll(a[:, 128:], 64, 1)


def layer_next(a):
    lo, r0, r1 = layer_rolls(a)
    return jnp.concatenate([jnp.where(lo, r0, r1), jnp.where(lo, r1, r0)], axis=1)


def layer_prev(a):
    lo, r0, r1 = layer_rolls(a)
    return jnp.concatenate([jnp.where(lo, r1, r0), jnp.where(lo, r0, r1)], axis=1)


def coupled(cross, vert, head):
    out = cross * cross_next(head) + cross_prev(cross * head)
    return out + vert * layer_next(head) + layer_prev(vert * head)


def reduce_chain(leak, face):
    n = len(leak)
    first, link, shunt = leak[0], face[0], leak[1]
    inv, ratio, share = [None] * n, [None] * n, [None] * n
    for i in range(1, n - 1):
        inv[i] = 1.0 / (face[i] + (shunt + link))
        ratio[i] = face[i] * inv[i]
        share[i] = link * inv[i]
        first = first + shunt * share[i]
        shunt = leak[i + 1] + shunt * ratio[i]
        link = link * ratio[i]
    return (inv, ratio, share), first, shunt, link


def reduce_source(ratio, share, rhs):
    n = len(rhs)
    first = rhs[0]
    part = [None] * n
    part[1] = rhs[1]
    for i in range(1, n - 1):
        first = first + share[i] * part[i]
        part[i + 1] = rhs[i + 1] + ratio[i] * part[i]
    return part, first, part[n - 1]


def fill_chain(coef, part, first, last):
    inv, ratio, share = coef
    n = len(ratio)
    out = [None] * n
    out[0], out[n - 1] = first, last
    for i in range(n - 2, 0, -1):
        value = share[i] * first + ratio[i] * out[i + 1]
        out[i] = value if part is None else value + inv[i] * part[i]
    return out


def full_factor(leak, face):
    n = len(leak)
    shunt = leak[0]
    inv, ratio = [None] * n, [None] * n
    for i in range(n - 1):
        inv[i] = 1.0 / (face[i] + shunt)
        ratio[i] = face[i] * inv[i]
        shunt = leak[i + 1] + shunt * ratio[i]
    inv[n - 1] = 1.0 / shunt
    return inv, ratio


def full_solve(inv, ratio, rhs):
    n = len(rhs)
    part = [rhs[0]]
    for i in range(n - 1):
        part.append(rhs[i + 1] + ratio[i] * part[i])
    out = [None] * n
    out[n - 1] = inv[n - 1] * part[n - 1]
    for i in range(n - 2, -1, -1):
        out[i] = inv[i] * part[i] + ratio[i] * out[i + 1]
    return out


def to_rows(a):
    return [a[k : k + 1] for k in range(SUBS)]


def interleave(a, b):
    return [x for pair in zip(to_rows(a), to_rows(b)) for x in pair]


def stack_ends(nodes):
    return jnp.concatenate(nodes[0::2], axis=0), jnp.concatenate(nodes[1::2], axis=0)


def column_sum(a):
    return jnp.sum(a, axis=0, keepdims=True)


def both(fn):
    return jnp.concatenate([fn(0), fn(1)], axis=1)


def step_rows(i):
    return pl.ds(i, SUBS, stride=STEPS)


def scatter_kernel(cells_ref, area_ref, land_ref, bmp_ref, rain_ref, table_ref, live_ref,
                   place_ref, first_ref, own_ref, second_ref, amount_ref, window_ref):
    slots = land_ref.shape[1]
    land = land_ref[...]
    rates = jnp.zeros((8, slots), F32)
    for use in range(table_ref.shape[1]):
        rates = jnp.where(land == use, table_ref[:, use : use + 1], rates)
    bmp = bmp_ref[...]
    chosen = jnp.zeros(bmp.shape, F32)
    for code in range(table_ref.shape[0]):
        chosen = jnp.where(bmp == code, rates[code : code + 1], chosen)
    alive = lax.broadcasted_iota(jnp.int32, (1, slots), 1) < live_ref[0]
    perc = jnp.where(alive, rain_ref[...] * chosen, 0.0)
    for q in range(4):
        amount = perc * area_ref[q : q + 1, :]
        high = amount.astype(BF16).astype(F32)
        amount_ref[q, 0:2, :] = high
        amount_ref[q, 2:4, :] = amount - high
    column = lax.broadcasted_iota(jnp.int32, (256, slots), 0).astype(F32).astype(BF16)
    line = lax.broadcasted_iota(jnp.int32, (96, slots), 0).astype(F32).astype(BF16)
    one, zero = jnp.ones((), BF16), jnp.zeros((), BF16)
    total = None
    for q in range(4):
        cell = cells_ref[q : q + 1, :]
        columns = jnp.where(column == (cell & 255).astype(F32).astype(BF16), one, zero)
        hit = line == (cell >> 8).astype(F32).astype(BF16)
        put = [jnp.where(hit, amount_ref[q, k : k + 1, :].astype(BF16), zero) for k in (0, 2, 1, 3)]
        product = lax.dot_general(
            jnp.concatenate(put, axis=0), columns, (((1,), (1,)), ((), ())), preferred_element_type=F32
        )
        total = product if total is None else total + product
    for s in range(2):
        summed = total[192 * s : 192 * s + 96] + total[192 * s + 96 : 192 * s + 192]
        for k in range(3):
            for odd in range(2):
                window_ref[k, pl.ds(64 * s + odd, 32, stride=2), :] = summed[
                    32 * k : 32 * k + 32, 128 * odd : 128 * odd + 128
                ]
    odd = lax.rem(place_ref[0], 2)
    own_ref[...] = window_ref[1].T
    first_ref[...] = window_ref[2 - 2 * odd].T
    second_ref[...] = window_ref[2 * odd].T


def coefficient_kernel(head_ref, storage_ref, flow_ref, cross_ref, vert_ref, active_ref,
                       fields_ref, small_ref, base_ref, gather_ref, turned):
    def turn(slot, part):
        for h in range(2):
            turned[slot, h] = part(h).T

    for slot, ref in enumerate((storage_ref, flow_ref, cross_ref, vert_ref)):
        turn(slot, lambda h: ref[2 * h : 2 * h + 2].reshape(128, 128))
    turn(4, lambda h: active_ref[2 * h : 2 * h + 2].reshape(128, 128).astype(F32))
    for s in range(2):
        turn(5 + s, lambda h: head_ref[s, 2 * h : 2 * h + 2].reshape(128, 128))

    def step(slot, i):
        return both(lambda h: turned[slot, h, step_rows(i), :])

    lane = lax.broadcasted_iota(jnp.int32, (SUBS, 256), 1)
    inner_cross = lane % 64 != 63
    inner_vert = lane < 192
    mask = [step(4, i) for i in range(STEPS)]
    leak, face, crosses, verts = [], [], [], []
    for i in range(STEPS):
        m = mask[i]
        cross = jnp.where(inner_cross, step(2, i) * m * cross_next(m), 0.0)
        vert = jnp.where(inner_vert, step(3, i) * m * layer_next(m), 0.0)
        store = step(0, i)
        leak.append(store + cross + cross_prev(cross) + vert + layer_prev(vert))
        after = mask[i + 1] if i + 1 < STEPS else pltpu.roll(mask[0], SUBS - 1, 0)
        face.append(step(1, i) * m * after)
        crosses.append(cross)
        verts.append(vert)
        fields_ref[0, i] = cross
        fields_ref[1, i] = vert
        fields_ref[2, i] = m
        for s in range(2):
            head = step(5 + s, i)
            base = store * head
            base_ref[s, i] = base
            base_ref[2 + s, i] = base + coupled(cross, vert, head)
    coef, first, last, link = reduce_chain(leak, face[: STEPS - 1])
    leak1 = interleave(first, last)
    face1 = interleave(link, face[STEPS - 1])[: 2 * SUBS - 1]
    coef1, first1, last1, link1 = reduce_chain(leak1, face1)
    for k in range(3):
        for i in range(1, STEPS - 1):
            fields_ref[3 + k, i] = coef[k][i]
        for i in range(1, 2 * SUBS - 1):
            small_ref[k, i : i + 1] = coef1[k][i]
    one, zero = jnp.ones((1, 256), F32), jnp.zeros((1, 256), F32)
    basis = []
    for ends in ((one, zero), (zero, one)):
        basis.append(fill_chain(coef, None, *stack_ends(fill_chain(coef1, None, *ends))))
    for k in range(2):
        for i in range(STEPS):
            fields_ref[6 + k, i] = basis[k][i]
    gather_ref[0:1] = first1
    gather_ref[1:2] = last1
    gather_ref[2:3] = link1
    gather_ref[3:4] = both(lambda h: turned[1, h, 127:128, :] * turned[4, h, 127:128, :])
    gather_ref[4:5] = both(lambda h: turned[4, h, 0:1, :])
    for row, weight, move in ((5, crosses, cross_next), (9, verts, layer_next)):
        sums = [jnp.zeros((SUBS, 256), F32)] * 4
        for i in range(STEPS):
            moved = [move(basis[k][i]) for k in range(2)]
            for a in range(2):
                weighted = weight[i] * basis[a][i]
                for b in range(2):
                    sums[2 * a + b] = sums[2 * a + b] + weighted * moved[b]
        for k in range(4):
            gather_ref[row + k : row + k + 1] = column_sum(sums[k])


def load_coef(fields_ref, small_ref):
    coef = tuple([None] + [fields_ref[3 + k, i] for i in range(1, STEPS - 1)] + [None] for k in range(3))
    coef1 = tuple([None] + [small_ref[k, i : i + 1] for i in range(1, 2 * SUBS - 1)] + [None] for k in range(3))
    return coef, coef1


def local_solve(coef, coef1, rhs, first, last):
    part, ends_first, ends_last = reduce_source(coef[1], coef[2], rhs)
    part1, source_first, source_last = reduce_source(coef1[1], coef1[2], interleave(ends_first, ends_last))
    ends = stack_ends(fill_chain(coef1, part1, first, last))
    return fill_chain(coef, part, *ends), source_first, source_last


def source_kernel(fields_ref, small_ref, base_ref, own_ref, low_ref, high_ref, coefs_ref,
                  source_ref, inner_ref, out_ref, rain_scratch):
    rain_scratch[...] = own_ref[...] + low_ref[...] + high_ref[...]
    coef, coef1 = load_coef(fields_ref, small_ref)
    top = lax.broadcasted_iota(jnp.int32, (SUBS, 128), 1) < 64
    zero = jnp.zeros((1, 256), F32)
    none = jnp.zeros((SUBS, 128), F32)
    rows = []
    for s in range(2):
        rhs = []
        for i in range(STEPS):
            water = rain_scratch[step_rows(i), :]
            if s:
                water = pltpu.roll(water, 64, 1)
            water = jnp.concatenate([jnp.where(top, water, 0.0), none], axis=1) * fields_ref[2, i]
            source_ref[s, i] = base_ref[s, i] + water
            rhs.append(base_ref[2 + s, i] + water)
        inner, first, last = local_solve(coef, coef1, rhs, zero, zero)
        sums = [jnp.zeros((SUBS, 256), F32)] * 2
        for i in range(STEPS):
            inner_ref[s, i] = inner[i]
            later = source_ref[s, i] + coupled(fields_ref[0, i], fields_ref[1, i], inner[i])
            for k in range(2):
                sums[k] = sums[k] + fields_ref[6 + k, i] * later
        rows += [first, last, column_sum(sums[0]), column_sum(sums[1])]
    put_block(out_ref, [coefs_ref[k : k + 1] for k in range(13)] + rows)


def put_block(ref, rows):
    for k in range(ROWS):
        row = rows[k] if k < len(rows) else jnp.zeros((1, 256), F32)
        for h in range(2):
            ref[ROWS * h + k : ROWS * h + k + 1] = row[:, 128 * h : 128 * h + 128]


def coupled_ends(got, later, low, high):
    for row, ahead, back in ((5, cross_next, cross_prev), (9, layer_next, layer_prev)):
        k = [got(row + m) for m in range(4)]
        low_ahead, high_ahead = ahead(low), ahead(high)
        later = (
            later[0] + k[0] * low_ahead + k[1] * high_ahead + back(k[0] * low + k[2] * high),
            later[1] + k[2] * low_ahead + k[3] * high_ahead + back(k[1] * low + k[3] * high),
        )
    return later


def member(blocks_ref, p):
    return lambda row: both(lambda h: blocks_ref[p, ROWS * h + row : ROWS * h + row + 1, :])


def group_later(blocks_ref, s, nodes):
    out = []
    for p in range(blocks_ref.shape[0]):
        got = member(blocks_ref, p)
        out += coupled_ends(got, (got(15 + 4 * s), got(16 + 4 * s)), nodes[2 * p], nodes[2 * p + 1])
    return out


def group_kernel(place_ref, own_ref, from1_ref, from3_ref, from2_ref, blocks_ref, saved_ref, out_ref, block):
    per = blocks_ref.shape[0]
    place = lax.rem(place_ref[0], per)
    for k, ref in ((0, own_ref), (1, from1_ref), (3, from3_ref), (2, from2_ref)):
        blocks_ref[lax.bitwise_xor(place, k)] = ref[...]
    got = [member(blocks_ref, p) for p in range(per)]
    leak, face = [], []
    for p in range(per):
        leak += [got[p](0), got[p](1)]
        face.append(got[p](2))
        if p + 1 < per:
            face.append(got[p](3) * got[p + 1](4))
    coef, first, last, link = reduce_chain(leak, face)
    nodes = 2 * per
    one, zero = jnp.ones((1, 256), F32), jnp.zeros((1, 256), F32)
    basis = [fill_chain(coef, None, one, zero), fill_chain(coef, None, zero, one)]
    for k in range(3):
        for i in range(1, nodes - 1):
            saved_ref[nodes * k + i : nodes * k + i + 1] = coef[k][i]
    rows = [first, last, link, got[per - 1](3), got[0](4)]
    for row, move in ((5, cross_next), (9, layer_next)):
        sums = [zero] * 4
        for p in range(per):
            moved = [[move(basis[b][2 * p + e]) for e in range(2)] for b in range(2)]
            k = [got[p](row + m) for m in range(4)]
            for b in range(2):
                ends = [k[2 * e] * moved[b][0] + k[2 * e + 1] * moved[b][1] for e in range(2)]
                for a in range(2):
                    sums[2 * a + b] = sums[2 * a + b] + basis[a][2 * p] * ends[0] + basis[a][2 * p + 1] * ends[1]
        rows += sums
    for s in range(2):
        rhs = [got[p](13 + 4 * s + e) for p in range(per) for e in range(2)]
        part, source_first, source_last = reduce_source(coef[1], coef[2], rhs)
        inner = fill_chain(coef, part, zero, zero)
        _, later_first, later_last = reduce_source(coef[1], coef[2], group_later(blocks_ref, s, inner))
        rows += [source_first, source_last, later_first, later_last]
        for i in range(nodes):
            saved_ref[nodes * (5 + s) + i : nodes * (5 + s) + i + 1] = inner[i]
            saved_ref[nodes * (3 + s) + i : nodes * (3 + s) + i + 1] = basis[s][i]
    put_block(block, rows)
    for k in range(out_ref.shape[0]):
        out_ref[k] = block[...]


def sweep_kernel(place_ref, gathered_ref, blocks_ref, saved_ref, fields_ref, small_ref, source_ref, inner_ref,
                 head_ref, total_ref, ends_scratch, turned):
    per = blocks_ref.shape[0]
    groups = gathered_ref.shape[0] // (2 * ROWS)
    place = place_ref[0]

    def got(row):
        return both(lambda h: gathered_ref[pl.ds(ROWS * h + row, groups, stride=2 * ROWS), :])

    face = got(3) * pltpu.roll(got(4), groups - 1, 0)
    inv, ratio = full_factor(interleave(got(0), got(1)), interleave(got(2), face)[: 2 * groups - 1])
    nodes = 2 * per
    saved = [[saved_ref[nodes * k + i : nodes * k + i + 1] for i in range(nodes)] for k in range(7)]
    at = pl.ds(place // per, 1)
    pick = pl.ds(lax.rem(place, per), 1)
    ends = []
    for s in range(2):
        row = 13 + 4 * s
        low, high = stack_ends(full_solve(inv, ratio, interleave(got(row), got(row + 1))))
        later = coupled_ends(got, (got(row + 2), got(row + 3)), low, high)
        low2, high2 = stack_ends(full_solve(inv, ratio, interleave(*later)))
        for k, value in enumerate((low, high, low2, high2)):
            ends_scratch[k] = value
        low, high, low2, high2 = [ends_scratch[k, at, :] for k in range(4)]
        first = [saved[5 + s][i] + saved[3][i] * low + saved[4][i] * high for i in range(nodes)]
        part, _, _ = reduce_source(saved[1], saved[2], group_later(blocks_ref, s, first))
        second = fill_chain(tuple(saved[:3]), part, low2, high2)
        for k, values in enumerate((first[0::2], first[1::2], second[0::2], second[1::2])):
            for p in range(per):
                ends_scratch[k, p : p + 1] = values[p]
        ends.append([ends_scratch[k, pick, :] for k in range(4)])
    coef, coef1 = load_coef(fields_ref, small_ref)
    for s in range(2):
        low1, high1, low2, high2 = ends[s]
        rhs = []
        for i in range(STEPS):
            head = inner_ref[s, i] + fields_ref[6, i] * low1 + fields_ref[7, i] * high1
            rhs.append(source_ref[s, i] + coupled(fields_ref[0, i], fields_ref[1, i], head))
        solved, _, _ = local_solve(coef, coef1, rhs, low2, high2)
        for i in range(STEPS):
            for h in range(2):
                turned[s, h, step_rows(i), :] = solved[i][:, 128 * h : 128 * h + 128]
    for h in range(2):
        lanes = [turned[s, h].T for s in range(2)]
        for s in range(2):
            head_ref[s, 2 * h : 2 * h + 2] = lanes[s].reshape(2, 64, 128)
        total_ref[2 * h : 2 * h + 2] = (lanes[0] + lanes[1]).reshape(2, 64, 128)


VMEM = pl.BlockSpec(memory_space=pltpu.VMEM)
SMEM = pl.BlockSpec(memory_space=pltpu.SMEM)


def kernel_call(body, name, specs, outs, scratch, flops):
    return pl.pallas_call(
        body,
        name=name,
        in_specs=specs,
        out_specs=[VMEM] * len(outs),
        out_shape=[jax.ShapeDtypeStruct(shape, F32) for shape in outs],
        scratch_shapes=[pltpu.VMEM(shape, F32) for shape in scratch],
        compiler_params=pltpu.CompilerParams(vmem_limit_bytes=48 * 2**20),
        cost_estimate=pl.CostEstimate(flops=flops, bytes_accessed=2 * 2**20, transcendentals=0),
    )


def on_device(
    head_prev,
    storage,
    cond_flow,
    cond_cross,
    cond_vert,
    active,
    hru_cells,
    hru_area,
    hru_land,
    hru_bmp,
    rain,
    perc_table,
    hru_live,
):
    slots = hru_land.shape[0]
    devices = lax.axis_size("flow")
    tile = (128, 128)
    blocks = [(4, slots), (4, slots), (1, slots), (2, slots), (1, slots), (8, 16)]
    place = lax.axis_index("flow").astype(jnp.int32).reshape(1)
    first, own, second = pl.pallas_call(
        scatter_kernel,
        name="scatter",
        grid=(1,),
        in_specs=[pl.BlockSpec(shape, lambda i: (0, 0)) for shape in blocks] + [SMEM] * 2,
        out_specs=[pl.BlockSpec(tile, lambda i: (0, 0))] * 3,
        out_shape=[jax.ShapeDtypeStruct(tile, F32)] * 3,
        scratch_shapes=[pltpu.VMEM((4, 4, slots), F32), pltpu.VMEM((3,) + tile, F32)],
        compiler_params=pltpu.CompilerParams(vmem_limit_bytes=60 * 2**20),
        cost_estimate=pl.CostEstimate(flops=4 * 10**9, bytes_accessed=2 * 2**20, transcendentals=0),
    )(
        hru_cells.T, hru_area.T, hru_land.reshape(1, slots), hru_bmp, rain.reshape(1, slots), perc_table.T, hru_live, place
    )
    low = lax.ppermute(second, "flow", [(i, i - 1 + 2 * (i % 2)) for i in range(1, devices - 1)])
    high = lax.ppermute(first, "flow", [(i, i ^ 1) for i in range(devices)])
    fields, small, base, coefs = kernel_call(
        coefficient_kernel,
        "coefficients",
        [VMEM] * 6,
        [(8, STEPS, SUBS, 256), (3, 2 * SUBS, 256), (4, STEPS, SUBS, 256), (16, 256)],
        [(7, 2, 128, 128)],
        4 * 10**9,
    )(head_prev, storage, cond_flow, cond_cross, cond_vert, active)
    source, inner, block = kernel_call(
        source_kernel,
        "sources",
        [VMEM] * 7,
        [(2, STEPS, SUBS, 256), (2, STEPS, SUBS, 256), (2 * ROWS, 128)],
        [tile],
        10**9,
    )(fields, small, base, own, low, high, coefs)
    per = devices // SUBS
    around = [
        lax.ppermute(block, "flow", [(i, i ^ k) for i in range(devices)]) for k in (1, 3, 2)
    ]
    blocks, saved, block = kernel_call(
        group_kernel,
        "groups",
        [SMEM] + [VMEM] * per,
        [(per, 2 * ROWS, 128), (14 * per, 256), (SUBS, 2 * ROWS, 128)],
        [(2 * ROWS, 128)],
        10**9,
    )(place, block, *around)
    same = [[i + per * k for k in range(SUBS)] for i in range(per)]
    gathered = lax.all_to_all(block, "flow", split_axis=0, concat_axis=0, axis_index_groups=same, tiled=True)
    head, total = kernel_call(
        sweep_kernel,
        "sweeps",
        [SMEM] + [VMEM] * 7,
        [head_prev.shape, storage.shape],
        [(4, SUBS, 256), (2, 2, 128, 128)],
        10**9,
    )(place, gathered.reshape(SUBS * 2 * ROWS, 128), blocks, saved, fields, small, source, inner)
    lanes = lax.axis_size("lane")
    whole = total
    for k in (2, 6, 4):
        whole = whole + lax.ppermute(total, "lane", [(i, i ^ k) for i in range(lanes)])
    whole = whole + lax.ppermute(whole, "lane", [(i, i ^ 1) for i in range(lanes)])
    anomaly = head - whole[None] / (2 * lanes)
    return head, anomaly


def solution(mesh):
    return jax.shard_map(
        on_device,
        mesh=mesh,
        in_specs=(
            P("lane", None, None, "flow"),
            P(None, None, "flow"),
            P(None, None, "flow"),
            P(None, None, "flow"),
            P(None, None, "flow"),
            P(None, None, "flow"),
            P("flow", None),
            P("flow", None),
            P("flow"),
            P("lane", "flow"),
            P("flow"),
            P(),
            P("flow"),
        ),
        out_specs=(P("lane", None, None, "flow"), P("lane", None, None, "flow")),
        check_vma=False,
    )
```

```python
import functools

import jax
import jax.numpy as jnp
from jax import lax
from jax.experimental import pallas as pl
from jax.experimental.pallas import tpu as pltpu
from jax.sharding import PartitionSpec as P

STEPS = 16
SUBS = 8
ROWS = 24
F32 = jnp.float32
BF16 = jnp.bfloat16


def halves(fn, a):
    return jnp.concatenate([fn(a[:, :128]), fn(a[:, 128:])], axis=1)


def cross_next(a):
    return halves(lambda h: pltpu.roll(h, 127, 1), a)


def cross_prev(a):
    return halves(lambda h: pltpu.roll(h, 1, 1), a)


def layer_rolls(a):
    lo = lax.broadcasted_iota(jnp.int32, (a.shape[0], 128), 1) < 64
    return lo, pltpu.roll(a[:, :128], 64, 1), pltpu.roll(a[:, 128:], 64, 1)


def layer_next(a):
    lo, r0, r1 = layer_rolls(a)
    return jnp.concatenate([jnp.where(lo, r0, r1), jnp.where(lo, r1, r0)], axis=1)


def layer_prev(a):
    lo, r0, r1 = layer_rolls(a)
    return jnp.concatenate([jnp.where(lo, r1, r0), jnp.where(lo, r0, r1)], axis=1)


def coupled(cross, vert, head):
    out = cross * cross_next(head) + cross_prev(cross * head)
    return out + vert * layer_next(head) + layer_prev(vert * head)


def reduce_chain(leak, face):
    n = len(leak)
    first, link, shunt = leak[0], face[0], leak[1]
    inv, ratio, share = [None] * n, [None] * n, [None] * n
    for i in range(1, n - 1):
        inv[i] = 1.0 / (face[i] + (shunt + link))
        ratio[i] = face[i] * inv[i]
        share[i] = link * inv[i]
        first = first + shunt * share[i]
        shunt = leak[i + 1] + shunt * ratio[i]
        link = link * ratio[i]
    return (inv, ratio, share), first, shunt, link


def reduce_source(ratio, share, rhs):
    n = len(rhs)
    first = rhs[0]
    part = [None] * n
    part[1] = rhs[1]
    for i in range(1, n - 1):
        first = first + share[i] * part[i]
        part[i + 1] = rhs[i + 1] + ratio[i] * part[i]
    return part, first, part[n - 1]


def fill_chain(coef, part, first, last):
    inv, ratio, share = coef
    n = len(ratio)
    out = [None] * n
    out[0], out[n - 1] = first, last
    for i in range(n - 2, 0, -1):
        value = share[i] * first + ratio[i] * out[i + 1]
        out[i] = value if part is None else value + inv[i] * part[i]
    return out


def full_factor(leak, face):
    n = len(leak)
    shunt = leak[0]
    inv, ratio = [None] * n, [None] * n
    for i in range(n - 1):
        inv[i] = 1.0 / (face[i] + shunt)
        ratio[i] = face[i] * inv[i]
        shunt = leak[i + 1] + shunt * ratio[i]
    inv[n - 1] = 1.0 / shunt
    return inv, ratio


def full_solve(inv, ratio, rhs):
    n = len(rhs)
    part = [rhs[0]]
    for i in range(n - 1):
        part.append(rhs[i + 1] + ratio[i] * part[i])
    out = [None] * n
    out[n - 1] = inv[n - 1] * part[n - 1]
    for i in range(n - 2, -1, -1):
        out[i] = inv[i] * part[i] + ratio[i] * out[i + 1]
    return out


def to_rows(a):
    return [a[k : k + 1] for k in range(SUBS)]


def interleave(a, b):
    return [x for pair in zip(to_rows(a), to_rows(b)) for x in pair]


def stack_ends(nodes):
    return jnp.concatenate(nodes[0::2], axis=0), jnp.concatenate(nodes[1::2], axis=0)


def column_sum(a):
    return jnp.sum(a, axis=0, keepdims=True)


def both(fn):
    return jnp.concatenate([fn(0), fn(1)], axis=1)


def step_rows(i):
    return pl.ds(i, SUBS, stride=STEPS)


def scatter_kernel(cells_ref, area_ref, land_ref, bmp_ref, rain_ref, table_ref, live_ref,
                   place_ref, first_ref, own_ref, second_ref, amount_ref, window_ref):
    slots = land_ref.shape[1]
    land = land_ref[...]
    rates = jnp.zeros((8, slots), F32)
    for use in range(table_ref.shape[1]):
        rates = jnp.where(land == use, table_ref[:, use : use + 1], rates)
    bmp = bmp_ref[...]
    chosen = jnp.zeros(bmp.shape, F32)
    for code in range(table_ref.shape[0]):
        chosen = jnp.where(bmp == code, rates[code : code + 1], chosen)
    alive = lax.broadcasted_iota(jnp.int32, (1, slots), 1) < live_ref[0]
    perc = jnp.where(alive, rain_ref[...] * chosen, 0.0)
    for q in range(4):
        amount = perc * area_ref[q : q + 1, :]
        high = amount.astype(BF16).astype(F32)
        amount_ref[q, 0:2, :] = high
        amount_ref[q, 2:4, :] = amount - high
    column = lax.broadcasted_iota(jnp.int32, (256, slots), 0).astype(F32).astype(BF16)
    line = lax.broadcasted_iota(jnp.int32, (96, slots), 0).astype(F32).astype(BF16)
    one, zero = jnp.ones((), BF16), jnp.zeros((), BF16)
    total = None
    for q in range(4):
        cell = cells_ref[q : q + 1, :]
        columns = jnp.where(column == (cell & 255).astype(F32).astype(BF16), one, zero)
        hit = line == (cell >> 8).astype(F32).astype(BF16)
        put = [jnp.where(hit, amount_ref[q, k : k + 1, :].astype(BF16), zero) for k in (0, 2, 1, 3)]
        product = lax.dot_general(
            jnp.concatenate(put, axis=0), columns, (((1,), (1,)), ((), ())), preferred_element_type=F32
        )
        total = product if total is None else total + product
    for s in range(2):
        summed = total[192 * s : 192 * s + 96] + total[192 * s + 96 : 192 * s + 192]
        for k in range(3):
            for odd in range(2):
                window_ref[k, pl.ds(64 * s + odd, 32, stride=2), :] = summed[
                    32 * k : 32 * k + 32, 128 * odd : 128 * odd + 128
                ]
    odd = lax.rem(place_ref[0], 2)
    own_ref[...] = window_ref[1].T
    first_ref[...] = window_ref[2 - 2 * odd].T
    second_ref[...] = window_ref[2 * odd].T


def coefficient_kernel(head_ref, storage_ref, flow_ref, cross_ref, vert_ref, active_ref,
                       fields_ref, small_ref, base_ref, gather_ref, turned):
    def turn(slot, part):
        for h in range(2):
            turned[slot, h] = part(h).T

    for slot, ref in enumerate((storage_ref, flow_ref, cross_ref, vert_ref)):
        turn(slot, lambda h: ref[2 * h : 2 * h + 2].reshape(128, 128))
    turn(4, lambda h: active_ref[2 * h : 2 * h + 2].reshape(128, 128).astype(F32))
    for s in range(2):
        turn(5 + s, lambda h: head_ref[s, 2 * h : 2 * h + 2].reshape(128, 128))

    def step(slot, i):
        return both(lambda h: turned[slot, h, step_rows(i), :])

    lane = lax.broadcasted_iota(jnp.int32, (SUBS, 256), 1)
    inner_cross = lane % 64 != 63
    inner_vert = lane < 192
    mask = [step(4, i) for i in range(STEPS)]
    leak, face, crosses, verts = [], [], [], []
    for i in range(STEPS):
        m = mask[i]
        cross = jnp.where(inner_cross, step(2, i) * m * cross_next(m), 0.0)
        vert = jnp.where(inner_vert, step(3, i) * m * layer_next(m), 0.0)
        store = step(0, i)
        leak.append(store + cross + cross_prev(cross) + vert + layer_prev(vert))
        after = mask[i + 1] if i + 1 < STEPS else pltpu.roll(mask[0], SUBS - 1, 0)
        face.append(step(1, i) * m * after)
        crosses.append(cross)
        verts.append(vert)
        fields_ref[0, i] = cross
        fields_ref[1, i] = vert
        fields_ref[2, i] = m
        for s in range(2):
            head = step(5 + s, i)
            base = store * head
            base_ref[s, i] = base
            base_ref[2 + s, i] = base + coupled(cross, vert, head)
    coef, first, last, link = reduce_chain(leak, face[: STEPS - 1])
    leak1 = interleave(first, last)
    face1 = interleave(link, face[STEPS - 1])[: 2 * SUBS - 1]
    coef1, first1, last1, link1 = reduce_chain(leak1, face1)
    for k in range(3):
        for i in range(1, STEPS - 1):
            fields_ref[3 + k, i] = coef[k][i]
        for i in range(1, 2 * SUBS - 1):
            small_ref[k, i : i + 1] = coef1[k][i]
    one, zero = jnp.ones((1, 256), F32), jnp.zeros((1, 256), F32)
    basis = []
    for ends in ((one, zero), (zero, one)):
        basis.append(fill_chain(coef, None, *stack_ends(fill_chain(coef1, None, *ends))))
    for k in range(2):
        for i in range(STEPS):
            fields_ref[6 + k, i] = basis[k][i]
    gather_ref[0:1] = first1
    gather_ref[1:2] = last1
    gather_ref[2:3] = link1
    gather_ref[3:4] = both(lambda h: turned[1, h, 127:128, :] * turned[4, h, 127:128, :])
    gather_ref[4:5] = both(lambda h: turned[4, h, 0:1, :])
    for row, weight, move in ((5, crosses, cross_next), (9, verts, layer_next)):
        sums = [jnp.zeros((SUBS, 256), F32)] * 4
        for i in range(STEPS):
            moved = [move(basis[k][i]) for k in range(2)]
            for a in range(2):
                weighted = weight[i] * basis[a][i]
                for b in range(2):
                    sums[2 * a + b] = sums[2 * a + b] + weighted * moved[b]
        for k in range(4):
            gather_ref[row + k : row + k + 1] = column_sum(sums[k])


def load_coef(fields_ref, small_ref):
    coef = tuple([None] + [fields_ref[3 + k, i] for i in range(1, STEPS - 1)] + [None] for k in range(3))
    coef1 = tuple([None] + [small_ref[k, i : i + 1] for i in range(1, 2 * SUBS - 1)] + [None] for k in range(3))
    return coef, coef1


def local_solve(coef, coef1, rhs, first, last):
    part, ends_first, ends_last = reduce_source(coef[1], coef[2], rhs)
    part1, source_first, source_last = reduce_source(coef1[1], coef1[2], interleave(ends_first, ends_last))
    ends = stack_ends(fill_chain(coef1, part1, first, last))
    return fill_chain(coef, part, *ends), source_first, source_last


def source_kernel(fields_ref, small_ref, base_ref, own_ref, low_ref, high_ref, coefs_ref,
                  source_ref, inner_ref, out_ref, rain_scratch):
    rain_scratch[...] = own_ref[...] + low_ref[...] + high_ref[...]
    coef, coef1 = load_coef(fields_ref, small_ref)
    top = lax.broadcasted_iota(jnp.int32, (SUBS, 128), 1) < 64
    zero = jnp.zeros((1, 256), F32)
    none = jnp.zeros((SUBS, 128), F32)
    rows = []
    for s in range(2):
        rhs = []
        for i in range(STEPS):
            water = rain_scratch[step_rows(i), :]
            if s:
                water = pltpu.roll(water, 64, 1)
            water = jnp.concatenate([jnp.where(top, water, 0.0), none], axis=1) * fields_ref[2, i]
            source_ref[s, i] = base_ref[s, i] + water
            rhs.append(base_ref[2 + s, i] + water)
        inner, first, last = local_solve(coef, coef1, rhs, zero, zero)
        sums = [jnp.zeros((SUBS, 256), F32)] * 2
        for i in range(STEPS):
            inner_ref[s, i] = inner[i]
            later = source_ref[s, i] + coupled(fields_ref[0, i], fields_ref[1, i], inner[i])
            for k in range(2):
                sums[k] = sums[k] + fields_ref[6 + k, i] * later
        rows += [first, last, column_sum(sums[0]), column_sum(sums[1])]
    put_block(out_ref, [coefs_ref[k : k + 1] for k in range(13)] + rows)


def put_block(ref, rows):
    for k in range(ROWS):
        row = rows[k] if k < len(rows) else jnp.zeros((1, 256), F32)
        for h in range(2):
            ref[ROWS * h + k : ROWS * h + k + 1] = row[:, 128 * h : 128 * h + 128]


def coupled_ends(got, later, low, high):
    for row, ahead, back in ((5, cross_next, cross_prev), (9, layer_next, layer_prev)):
        k = [got(row + m) for m in range(4)]
        low_ahead, high_ahead = ahead(low), ahead(high)
        later = (
            later[0] + k[0] * low_ahead + k[1] * high_ahead + back(k[0] * low + k[2] * high),
            later[1] + k[2] * low_ahead + k[3] * high_ahead + back(k[1] * low + k[3] * high),
        )
    return later


def member(blocks_ref, p):
    return lambda row: both(lambda h: blocks_ref[p, ROWS * h + row : ROWS * h + row + 1, :])


def group_later(blocks_ref, s, nodes):
    out = []
    for p in range(blocks_ref.shape[0]):
        got = member(blocks_ref, p)
        out += coupled_ends(got, (got(15 + 4 * s), got(16 + 4 * s)), nodes[2 * p], nodes[2 * p + 1])
    return out


def swaps(per):
    return (1, 3, 2) if per == 4 else (1,)


def in_order(blocks_ref, place, received):
    per = blocks_ref.shape[0]
    for k, ref in zip((0,) + swaps(per), received):
        blocks_ref[lax.bitwise_xor(place, k)] = ref[...]


def group_kernel(stride, place_ref, *refs):
    blocks_ref, saved_ref, out_ref = refs[-3:]
    per = blocks_ref.shape[0]
    in_order(blocks_ref, lax.rem(place_ref[0] // stride, per), refs[:per])
    got = [member(blocks_ref, p) for p in range(per)]
    leak, face = [], []
    for p in range(per):
        leak += [got[p](0), got[p](1)]
        face.append(got[p](2))
        if p + 1 < per:
            face.append(got[p](3) * got[p + 1](4))
    coef, first, last, link = reduce_chain(leak, face)
    nodes = 2 * per
    one, zero = jnp.ones((1, 256), F32), jnp.zeros((1, 256), F32)
    basis = [fill_chain(coef, None, one, zero), fill_chain(coef, None, zero, one)]
    for k in range(3):
        for i in range(1, nodes - 1):
            saved_ref[nodes * k + i : nodes * k + i + 1] = coef[k][i]
    rows = [first, last, link, got[per - 1](3), got[0](4)]
    for row, move in ((5, cross_next), (9, layer_next)):
        sums = [zero] * 4
        for p in range(per):
            moved = [[move(basis[b][2 * p + e]) for e in range(2)] for b in range(2)]
            k = [got[p](row + m) for m in range(4)]
            for b in range(2):
                ends = [k[2 * e] * moved[b][0] + k[2 * e + 1] * moved[b][1] for e in range(2)]
                for a in range(2):
                    sums[2 * a + b] = sums[2 * a + b] + basis[a][2 * p] * ends[0] + basis[a][2 * p + 1] * ends[1]
        rows += sums
    for s in range(2):
        rhs = [got[p](13 + 4 * s + e) for p in range(per) for e in range(2)]
        part, source_first, source_last = reduce_source(coef[1], coef[2], rhs)
        inner = fill_chain(coef, part, zero, zero)
        _, later_first, later_last = reduce_source(coef[1], coef[2], group_later(blocks_ref, s, inner))
        rows += [source_first, source_last, later_first, later_last]
        for i in range(nodes):
            saved_ref[nodes * (5 + s) + i : nodes * (5 + s) + i + 1] = inner[i]
            saved_ref[nodes * (3 + s) + i : nodes * (3 + s) + i + 1] = basis[s][i]
    put_block(out_ref, rows)


def sweep_kernel(strides, place_ref, *refs):
    top = refs[-3].shape[0]
    blocks1_ref, saved1_ref, blocks2_ref, saved2_ref, fields_ref, small_ref, source_ref, inner_ref = refs[top : top + 8]
    head_ref, total_ref, top_ref, ends_scratch, turned = refs[top + 8 :]
    place = place_ref[0]
    side = place // strides[2]
    in_order(top_ref, side, refs[:top])
    got = [member(top_ref, p) for p in range(top)]
    face = []
    for p in range(top):
        face.append(got[p](2))
        if p + 1 < top:
            face.append(got[p](3) * got[p + 1](4))
    inv, ratio = full_factor([got[p](e) for p in range(top) for e in range(2)], face)
    levels = []
    for stride, blocks_ref, saved_ref in ((strides[1], blocks2_ref, saved2_ref), (strides[0], blocks1_ref, saved1_ref)):
        nodes = 2 * blocks_ref.shape[0]
        rows = [[saved_ref[nodes * k + i : nodes * k + i + 1] for i in range(nodes)] for k in range(7)]
        levels.append((blocks_ref, rows, pl.ds(lax.rem(place // stride, blocks_ref.shape[0]), 1)))

    def pick(first, second, at):
        for k, values in enumerate((first[0::2], first[1::2], second[0::2], second[1::2])):
            for p in range(len(values)):
                ends_scratch[k, p : p + 1] = values[p]
        return [ends_scratch[k, at, :] for k in range(4)]

    ends = []
    for s in range(2):
        first = full_solve(inv, ratio, [got[p](13 + 4 * s + e) for p in range(top) for e in range(2)])
        second = full_solve(inv, ratio, group_later(top_ref, s, first))
        low, high, low2, high2 = pick(first, second, pl.ds(side, 1))
        for blocks_ref, saved, at in levels:
            nodes = 2 * blocks_ref.shape[0]
            first = [saved[5 + s][i] + saved[3][i] * low + saved[4][i] * high for i in range(nodes)]
            part, _, _ = reduce_source(saved[1], saved[2], group_later(blocks_ref, s, first))
            second = fill_chain(tuple(saved[:3]), part, low2, high2)
            low, high, low2, high2 = pick(first, second, at)
        ends.append((low, high, low2, high2))
    coef, coef1 = load_coef(fields_ref, small_ref)
    for s in range(2):
        low1, high1, low2, high2 = ends[s]
        rhs = []
        for i in range(STEPS):
            head = inner_ref[s, i] + fields_ref[6, i] * low1 + fields_ref[7, i] * high1
            rhs.append(source_ref[s, i] + coupled(fields_ref[0, i], fields_ref[1, i], head))
        solved, _, _ = local_solve(coef, coef1, rhs, low2, high2)
        for i in range(STEPS):
            for h in range(2):
                turned[s, h, step_rows(i), :] = solved[i][:, 128 * h : 128 * h + 128]
    for h in range(2):
        lanes = [turned[s, h].T for s in range(2)]
        for s in range(2):
            head_ref[s, 2 * h : 2 * h + 2] = lanes[s].reshape(2, 64, 128)
        total_ref[2 * h : 2 * h + 2] = (lanes[0] + lanes[1]).reshape(2, 64, 128)


VMEM = pl.BlockSpec(memory_space=pltpu.VMEM)
SMEM = pl.BlockSpec(memory_space=pltpu.SMEM)


def kernel_call(body, name, specs, outs, scratch, flops):
    return pl.pallas_call(
        body,
        name=name,
        in_specs=specs,
        out_specs=[VMEM] * len(outs),
        out_shape=[jax.ShapeDtypeStruct(shape, F32) for shape in outs],
        scratch_shapes=[pltpu.VMEM(shape, F32) for shape in scratch],
        compiler_params=pltpu.CompilerParams(vmem_limit_bytes=48 * 2**20),
        cost_estimate=pl.CostEstimate(flops=flops, bytes_accessed=2 * 2**20, transcendentals=0),
    )


def on_device(
    head_prev,
    storage,
    cond_flow,
    cond_cross,
    cond_vert,
    active,
    hru_cells,
    hru_area,
    hru_land,
    hru_bmp,
    rain,
    perc_table,
    hru_live,
):
    slots = hru_land.shape[0]
    devices = lax.axis_size("flow")
    tile = (128, 128)
    blocks = [(4, slots), (4, slots), (1, slots), (2, slots), (1, slots), (8, 16)]
    place = lax.axis_index("flow").astype(jnp.int32).reshape(1)
    first, own, second = pl.pallas_call(
        scatter_kernel,
        name="scatter",
        grid=(1,),
        in_specs=[pl.BlockSpec(shape, lambda i: (0, 0)) for shape in blocks] + [SMEM] * 2,
        out_specs=[pl.BlockSpec(tile, lambda i: (0, 0))] * 3,
        out_shape=[jax.ShapeDtypeStruct(tile, F32)] * 3,
        scratch_shapes=[pltpu.VMEM((4, 4, slots), F32), pltpu.VMEM((3,) + tile, F32)],
        compiler_params=pltpu.CompilerParams(vmem_limit_bytes=60 * 2**20),
        cost_estimate=pl.CostEstimate(flops=4 * 10**9, bytes_accessed=2 * 2**20, transcendentals=0),
    )(
        hru_cells.T, hru_area.T, hru_land.reshape(1, slots), hru_bmp, rain.reshape(1, slots), perc_table.T, hru_live, place
    )
    low = lax.ppermute(second, "flow", [(i, i - 1 + 2 * (i % 2)) for i in range(1, devices - 1)])
    high = lax.ppermute(first, "flow", [(i, i ^ 1) for i in range(devices)])
    fields, small, base, coefs = kernel_call(
        coefficient_kernel,
        "coefficients",
        [VMEM] * 6,
        [(8, STEPS, SUBS, 256), (3, 2 * SUBS, 256), (4, STEPS, SUBS, 256), (16, 256)],
        [(7, 2, 128, 128)],
        4 * 10**9,
    )(head_prev, storage, cond_flow, cond_cross, cond_vert, active)
    source, inner, block = kernel_call(
        source_kernel,
        "sources",
        [VMEM] * 7,
        [(2, STEPS, SUBS, 256), (2, STEPS, SUBS, 256), (2 * ROWS, 128)],
        [tile],
        10**9,
    )(fields, small, base, own, low, high, coefs)
    sizes = (4, 4, 2)
    strides = (1, 4, 16)
    levels = []
    for stride, per in zip(strides, sizes):
        size = stride * per
        around = [
            lax.ppermute(block, "flow", [(i, i ^ (k * stride)) for i in range(devices)]) for k in swaps(per)
        ]
        if size == devices:
            break
        blocks, saved, block = kernel_call(
            functools.partial(group_kernel, stride),
            "groups",
            [SMEM] + [VMEM] * per,
            [(per, 2 * ROWS, 128), (14 * per, 256), (2 * ROWS, 128)],
            [],
            10**9,
        )(place, block, *around)
        levels += [blocks, saved]
    head, total = kernel_call(
        functools.partial(sweep_kernel, strides),
        "sweeps",
        [SMEM] + [VMEM] * (sizes[2] + 8),
        [head_prev.shape, storage.shape],
        [(sizes[2], 2 * ROWS, 128), (4, SUBS, 256), (2, 2, 128, 128)],
        10**9,
    )(place, block, *around, *levels, fields, small, source, inner)
    lanes = lax.axis_size("lane")
    whole = total
    for k in (2, 6, 4):
        whole = whole + lax.ppermute(total, "lane", [(i, i ^ k) for i in range(lanes)])
    whole = whole + lax.ppermute(whole, "lane", [(i, i ^ 1) for i in range(lanes)])
    anomaly = head - whole[None] / (2 * lanes)
    return head, anomaly


def solution(mesh):
    return jax.shard_map(
        on_device,
        mesh=mesh,
        in_specs=(
            P("lane", None, None, "flow"),
            P(None, None, "flow"),
            P(None, None, "flow"),
            P(None, None, "flow"),
            P(None, None, "flow"),
            P(None, None, "flow"),
            P("flow", None),
            P("flow", None),
            P("flow"),
            P("lane", "flow"),
            P("flow"),
            P(),
            P("flow"),
        ),
        out_specs=(P("lane", None, None, "flow"), P("lane", None, None, "flow")),
        check_vma=False,
    )
```
